128 devices in a mesh: dev: 128 (over z, y, x, core).
Axes of the slice: x: 4, y: 4, z: 4, core: 2. Of those that a mesh axis runs over, the one named last changes fastest.
Arguments:
- tokens: bfloat16 [2, 25216, 768], P(None, 'dev'), may hold values from -24 to 24
- cotangent: float32 [2, 25216, 768], P(None, 'dev'), may hold values from -6 to 6
- routes: int32 [2, 25216, 2], P(None, 'dev'), may hold values from 0 to 2, all different within a row; in each aligned block of 197 rows (0 to 196, 197 to 393, ..., all dimensions but the last counted through in order) at most 133 rows name the same one
- qkv_weight: bfloat16 [768, 2304], P('dev'), may hold values from -0.21875 to 0.21875
- out_weight: bfloat16 [768, 768], P('dev'), may hold values from -2 to 2
- norm_gain: bfloat16 [2, 768], P(None, 'dev'), may hold values from 0.5 to 1.5
- bias_rows: bfloat16 [5, 768], P(None, 'dev'), may hold values from -0.59765625 to 0.59765625
- router_weight: bfloat16 [768, 3], P('dev'), may hold values from -0.15625 to 0.15625
- expand_weight: bfloat16 [3, 768, 3072], P(None, 'dev'), may hold values from -0.21875 to 0.21875
- shrink_weight: bfloat16 [3, 3072, 768], P(None, 'dev'), may hold values from -0.21875 to 0.21875
- expert_bias: bfloat16 [3, 3840], P(None, 'dev'), may hold values from -0.59765625 to 0.59765625
- first_qkv: float32 [768, 2304], P('dev'), may hold values from -192 to 192
- first_out: float32 [768, 768], P('dev'), may hold values from -28 to 28
- first_gain: float32 [2, 768], P(None, 'dev'), may hold values from -320 to 320
- first_bias: float32 [5, 768], P(None, 'dev'), may hold values from -256 to 256
- first_router: float32 [768, 3], P('dev'), may hold values from -1536 to 1536
- first_expand: float32 [3, 768, 3072], P(None, 'dev'), may hold values from -40 to 40
- first_shrink: float32 [3, 3072, 768], P(None, 'dev'), may hold values from -40 to 40
- first_expert: float32 [3, 3840], P(None, 'dev'), may hold values from -56 to 56
- second_qkv: float32 [768, 2304], P('dev'), may hold values from 5043.2 to 20172.8
- second_out: float32 [768, 768], P('dev'), may hold values from 84.48 to 332.8
- second_gain: float32 [2, 768], P(None, 'dev'), may hold values from 12608 to 50432
- second_bias: float32 [5, 768], P(None, 'dev'), may hold values from 7564.8 to 30259.2
- second_router: float32 [768, 3], P('dev'), may hold values from 251756.55 to 1007026.2
- second_expand: float32 [3, 768, 3072], P(None, 'dev'), may hold values from 163.904 to 668.224
- second_shrink: float32 [3, 3072, 768], P(None, 'dev'), may hold values from 191.6416 to 756.48
- second_expert: float32 [3, 3840], P(None, 'dev'), may hold values from 327.808 to 1311.232
Outputs:
- output: float32 [2, 25216, 768], P(None, 'dev')
- input_grad: float32 [2, 25216, 768], P(None, 'dev')
- qkv_first: float32 [768, 2304], P('dev')
- qkv_second: float32 [768, 2304], P('dev')
- qkv_new: float32 [768, 2304], P('dev')
- out_first: float32 [768, 768], P('dev')
- out_second: float32 [768, 768], P('dev')
- out_new: float32 [768, 768], P('dev')
- gain_first: float32 [2, 768], P(None, 'dev')
- gain_second: float32 [2, 768], P(None, 'dev')
- gain_new: float32 [2, 768], P(None, 'dev')
- bias_first: float32 [5, 768], P(None, 'dev')
- bias_second: float32 [5, 768], P(None, 'dev')
- bias_new: float32 [5, 768], P(None, 'dev')
- router_first: float32 [768, 3], P('dev')
- router_second: float32 [768, 3], P('dev')
- router_new: float32 [768, 3], P('dev')
- expand_first: float32 [3, 768, 3072], P(None, 'dev')
- expand_second: float32 [3, 768, 3072], P(None, 'dev')
- expand_new: float32 [3, 768, 3072], P(None, 'dev')
- shrink_first: float32 [3, 3072, 768], P(None, 'dev')
- shrink_second: float32 [3, 3072, 768], P(None, 'dev')
- shrink_new: float32 [3, 3072, 768], P(None, 'dev')
- expert_first: float32 [3, 3840], P(None, 'dev')
- expert_second: float32 [3, 3840], P(None, 'dev')
- expert_new: float32 [3, 3840], P(None, 'dev')
The draws below stay inside these ranges and needn't reach their ends.
Inputs may be any that keep to these rules, and one draw needn't show every extreme that they name: `routes`: each token names 2 different experts. In each aligned block of 197 tokens (one device's tokens of one micro-batch) no expert is named by more than 133 tokens, and in some block one expert is named by exactly 133.
All inputs are finite; a program needn't handle non-finite values.
Results may differ from the reference program's by a relative error of at most 0.015.
Values may be sent and summed in bfloat16 or wider, within the bound.
No kernel may reach another device: no remote copies, remote signals or barrier semaphores. Data moves between devices by JAX's collectives and lax.ppermute only.
A program may use at most 384 MiB of HBM per device.

```python
import math
import jax
import jax.numpy as jnp
import numpy as np
from jax import lax

D = 768
HEADS = 12
HEAD = 64
FF = 3072
EXPERTS = 3
TOP = 2
SEQ = 197
MICRO = 2
STEP = 10
ROWS = 197
TOK_MB = 25216
CAP = 133


def strengthened(values, key, source, target, parts, factor):
    owner, partner = [(jnp.arange(values.shape[dim]) // (values.shape[dim] // parts)).reshape([-1 if axis == dim else 1 for axis in range(values.ndim)]) for dim in (source, target)]
    chosen = jax.random.permutation(key, parts)[partner]
    strong = (owner == chosen) | (owner == (partner + parts // 2) % parts)
    return jnp.where(strong, factor * values, values)


def shard_levels(stream_key, dims, split, smallest, high):
    loudness = 1.0
    for dim, shards_of in split:
        heights = jax.random.uniform(jax.random.fold_in(jax.random.fold_in(stream_key, 6), dim), (shards_of,), jnp.float32, smallest / len(split), high / len(split))
        loudness = loudness * jnp.repeat(jnp.exp(heights), dims[dim] // shards_of).reshape((-1,) + (1,) * (len(dims) - 1 - dim))
    return loudness


def routed_block(stream_key, own, number, rows, amount, top, reach, skew):
    order = jax.random.permutation(stream_key, amount)
    heavy_load, usual = portions_of(amount, rows * top, reach, skew, True), portions_of(amount, rows * top, reach, skew, False)
    places = jnp.arange(amount)

    def named(tallies, rotation):
        used = int((tallies > 0).sum())
        fixed = max(1, used // 4)
        passed = fixed + (places - fixed + rotation * (used - fixed)) % max(1, amount - fixed)
        return jnp.zeros((amount,), jnp.int32).at[order[jnp.where(places < fixed, places, passed)]].set(jnp.asarray(tallies, jnp.int32))

    tallies = jnp.where(number % 4 == 0, named(heavy_load, number // 4), named(usual, number - number // 4 - 1))
    mixed = jax.random.permutation(jax.random.fold_in(own, 3), amount)
    source_of, receiver = mixed[0:amount // 2 * 2:2], mixed[1:amount // 2 * 2:2]
    slack = jnp.minimum(tallies[source_of] - 1, reach - tallies[receiver]) // 2
    slack = jnp.where((source_of == order[0]) | (receiver == order[0]) | (tallies[receiver] == 0), 0, jnp.maximum(slack, 0))
    passed = jax.random.randint(jax.random.fold_in(own, 4), (amount // 2,), 0, 1 << 20) % (slack + 1)
    tallies = tallies.at[source_of].add(-passed).at[receiver].add(passed)
    members = jnp.searchsorted(jnp.cumsum(tallies), jnp.arange(rows * top), side="right").astype(jnp.int32)
    grid = members.reshape(top, rows).T
    grid = grid[jax.random.permutation(jax.random.fold_in(own, 1), rows)]
    rotation = jax.random.randint(jax.random.fold_in(own, 2), (rows, 1), 0, top)
    return jnp.take_along_axis(grid, (jnp.arange(top)[None, :] + rotation) % top, axis=1)


def portions_of(count, total, most, skew, full):
    weights = [(1 << 20) // math.isqrt(grade ** skew) + 1 for grade in range(1, count + 1)]
    largest = most if full else min(most, max(-(-total // count), total * weights[0] // sum(weights)))
    least = 1 if total - largest >= count - 1 else 0
    given, spare = [largest] + [least] * (count - 1), total - largest - least * (count - 1)
    while spare > 0:
        candidates = [i for i in range(1, count) if given[i] < largest] or [i for i in range(1, count) if given[i] < most]
        mass, left = sum([weights[i] for i in candidates]), spare
        for i in candidates:
            extra = min(most - given[i], max(1, left * weights[i] // mass), spare)
            given[i] = given[i] + extra
            spare = spare - extra
    return np.array(given)


def gaussian(key, shape, scale, most, split=(), held_as=jnp.bfloat16):
    drawn = scale * jax.random.normal(key, shape, jnp.float32)
    if split:
        drawn = drawn * shard_levels(key, shape, split, -0.22, 0.18)
    return jnp.clip(drawn, -most, most).astype(held_as)


def heavy_noise(stream_key, shape, deviation, reach, pieces, heavy, held_as=jnp.bfloat16):
    entries = deviation * jax.random.normal(stream_key, shape, jnp.float32)
    if pieces:
        entries = entries * shard_levels(stream_key, shape, pieces, -0.22, 0.18)
    return jnp.clip(strengthened(entries, jax.random.fold_in(stream_key, 3), *heavy), -reach, reach).astype(held_as)


def setup_inputs(seed: int = 0) -> dict:
    key_of = jax.random.split(jax.random.key(seed), 28)
    tokens = heavy_noise(key_of[0], (MICRO, TOK_MB, D), 1.0, 24.0, ((1, 128),), (1, 2, 128, 5.5))
    cotangent = gaussian(key_of[1], (MICRO, TOK_MB, D), 1.0, 6.0, ((1, 128),), jnp.float32)
    routes_keys = jax.random.split(jax.random.fold_in(key_of[2], 1), MICRO * TOK_MB // ROWS)
    routes_turns = jax.random.permutation(jax.random.fold_in(key_of[2], 3), MICRO * TOK_MB // ROWS)
    routes = jax.vmap(lambda own, number: routed_block(jax.random.fold_in(key_of[2], 2), own, number, ROWS, EXPERTS, TOP, CAP, 0))(routes_keys, routes_turns).reshape((MICRO, TOK_MB, TOP))
    qkv_weight = gaussian(key_of[3], (D, 3 * D), D ** -0.5, 0.21875, ((0, 128),))
    out_weight = gaussian(key_of[4], (D, D), (3 * (D // SEQ)) ** -0.5, 2.0, ((0, 128),))
    norm_gain = jnp.clip(1.0 + 0.1 * jax.random.normal(key_of[5], (2, D), jnp.float32), 0.5, 1.5).astype(jnp.bfloat16)
    bias_rows = gaussian(key_of[6], (5, D), 0.1, 0.59765625, ((1, 128),))
    router_weight = gaussian(key_of[7], (D, EXPERTS), (2 * D) ** -0.5, 0.15625, ((0, 128),))
    expand_weight = gaussian(key_of[8], (EXPERTS, D, FF), D ** -0.5, 0.21875, ((1, 128),))
    shrink_weight = gaussian(key_of[9], (EXPERTS, FF, D), (FF // 4) ** -0.5, 0.21875, ((1, 128),))
    expert_bias = gaussian(key_of[10], (EXPERTS, FF + D), 0.1, 0.59765625, ((1, 128),))
    first_qkv = gaussian(key_of[11], (D, 3 * D), (0.15 * (MICRO * TOK_MB) ** 0.5), 192.0, ((0, 128),), jnp.float32)
    first_out = gaussian(key_of[12], (D, D), (0.28 * (MICRO * TOK_MB // SEQ) ** 0.5), 28.0, ((0, 128),), jnp.float32)
    first_gain = gaussian(key_of[13], (2, D), (0.24 * (MICRO * TOK_MB) ** 0.5), 320.0, ((1, 128),), jnp.float32)
    first_bias = gaussian(key_of[14], (5, D), (0.19 * (MICRO * TOK_MB) ** 0.5), 256.0, ((1, 128),), jnp.float32)
    first_router = gaussian(key_of[15], (D, EXPERTS), (0.04 * (D * MICRO * TOK_MB) ** 0.5), 1536.0, ((0, 128),), jnp.float32)
    first_expand = gaussian(key_of[16], (EXPERTS, D, FF), (0.055 * (MICRO * TOK_MB * D // FF) ** 0.5), 40.0, ((1, 128),), jnp.float32)
    first_shrink = gaussian(key_of[17], (EXPERTS, FF, D), (0.03 * (MICRO * TOK_MB) ** 0.5), 40.0, ((1, 128),), jnp.float32)
    first_expert = gaussian(key_of[18], (EXPERTS, FF + D), (0.039 * (MICRO * TOK_MB) ** 0.5), 56.0, ((1, 128),), jnp.float32)
    second_qkv = jnp.clip(jnp.exp(math.log(20172.8) - 1.3862944 * jax.random.uniform(key_of[19], (D, 3 * D), jnp.float32) ** shard_levels(key_of[19], (D, 3 * D), ((0, 128),), -0.2, 0.2)), 5043.2, 20172.8)
    second_out = jnp.clip(jnp.exp(math.log(332.8) - 1.3710268 * jax.random.uniform(key_of[20], (D, D), jnp.float32) ** shard_levels(key_of[20], (D, D), ((0, 128),), -0.2, 0.2)), 84.48, 332.8)
    second_gain = jnp.clip(jnp.exp(math.log(50432.0) - 1.3862944 * jax.random.uniform(key_of[21], (2, D), jnp.float32) ** shard_levels(key_of[21], (2, D), ((1, 128),), -0.2, 0.2)), 12608.0, 50432.0)
    second_bias = jnp.clip(jnp.exp(math.log(30259.2) - 1.3862944 * jax.random.uniform(key_of[22], (5, D), jnp.float32) ** shard_levels(key_of[22], (5, D), ((1, 128),), -0.2, 0.2)), 7564.8, 30259.2)
    second_router = jnp.clip(jnp.exp(math.log(1007026.2) - 1.3862944 * jax.random.uniform(key_of[23], (D, EXPERTS), jnp.float32) ** shard_levels(key_of[23], (D, EXPERTS), ((0, 128),), -0.2, 0.2)), 251756.55, 1007026.2)
    second_expand = jnp.clip(jnp.exp(math.log(668.224) - 1.4053425 * jax.random.uniform(key_of[24], (EXPERTS, D, FF), jnp.float32) ** shard_levels(key_of[24], (EXPERTS, D, FF), ((1, 128),), -0.2, 0.2)), 163.904, 668.224)
    second_shrink = jnp.clip(jnp.exp(math.log(756.48) - 1.3730491 * jax.random.uniform(key_of[25], (EXPERTS, FF, D), jnp.float32) ** shard_levels(key_of[25], (EXPERTS, FF, D), ((1, 128),), -0.2, 0.2)), 191.6416, 756.48)
    second_expert = jnp.clip(jnp.exp(math.log(1311.232) - 1.3862944 * jax.random.uniform(key_of[26], (EXPERTS, FF + D), jnp.float32) ** shard_levels(key_of[26], (EXPERTS, FF + D), ((1, 128),), -0.2, 0.2)), 327.808, 1311.232)
    return dict(tokens=tokens, cotangent=cotangent, routes=routes, qkv_weight=qkv_weight, out_weight=out_weight, norm_gain=norm_gain, bias_rows=bias_rows, router_weight=router_weight, expand_weight=expand_weight, shrink_weight=shrink_weight, expert_bias=expert_bias, first_qkv=first_qkv, first_out=first_out, first_gain=first_gain, first_bias=first_bias, first_router=first_router, first_expand=first_expand, first_shrink=first_shrink, first_expert=first_expert, second_qkv=second_qkv, second_out=second_out, second_gain=second_gain, second_bias=second_bias, second_router=second_router, second_expand=second_expand, second_shrink=second_shrink, second_expert=second_expert)


@jax.custom_vjp
def low(v):
    return lax.optimization_barrier(v.astype(jnp.bfloat16)).astype(jnp.float32)

@jax.custom_vjp
def low_back(v):
    return v

def low_keep(v):
    return (low(v), None)

def low_pass(kept, grad):
    return (grad,)

def back_keep(v):
    return (v, None)

def back_low(kept, grad):
    return (low(grad),)
low.defvjp(low_keep, low_pass)
low_back.defvjp(back_keep, back_low)
NORM_EPS = 1e-06
ADAM_EPS = 1e-08
BETA_ONE = 0.9
BETA_TWO = 0.95
ROOT_HALF = 0.7071067811865476
RATES = (0.04, 0.2, 0.4, 0.04, 0.03, 0.04, 0.05, 0.04)
DECAYS = (0.1, 0.1, 0.0, 0.0, 0.1, 0.1, 0.1, 0.0)
PRECISE = lax.Precision.HIGHEST

def layer_norm(values, gain_row, shift_row):
    average = lax.optimization_barrier(jnp.mean(values, -1, keepdims=True))
    centred = values - average
    return centred * lax.rsqrt(lax.optimization_barrier(jnp.mean(centred * centred, -1, keepdims=True)) + NORM_EPS) * gain_row + shift_row

def softmax_rows(logits):
    shifted = jnp.exp(logits - lax.optimization_barrier(jnp.max(logits, -1, keepdims=True)))
    return shifted / lax.optimization_barrier(jnp.sum(shifted, -1, keepdims=True))

def gelu_exact(hidden):
    return hidden * 0.5 * (1.0 + lax.erf(hidden * ROOT_HALF))

def block(params, rows_in, route_rows):
    qkv_weight, out_weight, norm_gain, bias_rows, router_weight, expand_weight, shrink_weight, expert_bias = params
    images = rows_in.shape[0]
    model_width = rows_in.shape[2]
    experts_count = router_weight.shape[1]
    hidden_width = expand_weight.shape[2]
    scaling = HEAD ** (-0.5)
    attn_input = low(layer_norm(rows_in, norm_gain[0], bias_rows[0]))
    qkv_bias = jnp.concatenate([bias_rows[2], jnp.zeros_like(bias_rows[2]), bias_rows[3]])
    qkv_rows = low_back(low(jnp.einsum('isd,de->ise', attn_input, qkv_weight, precision=PRECISE) + qkv_bias))
    split_rows = qkv_rows.reshape(images, SEQ, 3, HEADS, HEAD)
    queries = split_rows[:, :, 0]
    key_rows = split_rows[:, :, 1]
    values = split_rows[:, :, 2]
    scores = low_back(jnp.einsum('iqhc,ikhc->ihqk', queries, key_rows, precision=PRECISE) * scaling)
    weights = low(softmax_rows(scores))
    attended = jnp.einsum('ihqk,ikhc->iqhc', weights, values, precision=PRECISE).reshape(images, SEQ, model_width)
    attended = low_back(low(attended))
    branch = low_back(jnp.einsum('isd,de->ise', attended, out_weight, precision=PRECISE) + bias_rows[4])
    middle = rows_in + branch
    expert_input = low(layer_norm(middle, norm_gain[1], bias_rows[1]))
    logits = low_back(jnp.einsum('isd,de->ise', expert_input, router_weight, precision=PRECISE))
    router_prob = softmax_rows(logits)
    onehot = (route_rows[..., None] == jnp.arange(experts_count, dtype=jnp.int32)).astype(jnp.float32)
    picked = lax.optimization_barrier(jnp.sum(onehot * router_prob[:, :, None, :], -1))
    gate_share = picked / lax.optimization_barrier(jnp.sum(picked, -1, keepdims=True))
    combine = lax.optimization_barrier(jnp.sum(onehot * gate_share[..., None], 2))
    mixed = middle
    for expert in range(experts_count):
        hidden_pre = jnp.einsum('isd,df->isf', expert_input, expand_weight[expert], precision=PRECISE)
        hidden_pre = low_back(hidden_pre + expert_bias[expert, :hidden_width])
        activated = low(gelu_exact(hidden_pre))
        expert_rows = jnp.einsum('isf,fd->isd', activated, shrink_weight[expert], precision=PRECISE)
        expert_rows = low_back(expert_rows + expert_bias[expert, hidden_width:])
        mixed = mixed + combine[:, :, expert:expert + 1] * expert_rows
    return mixed

def adam_update(weight, gradient, first_old, second_old, rate_value, decay_rate):
    first_new = BETA_ONE * first_old + (1.0 - BETA_ONE) * gradient
    second_new = BETA_TWO * second_old + (1.0 - BETA_TWO) * gradient * gradient
    weight_full = weight.astype(jnp.float32)
    ratio = first_new / (1.0 - BETA_ONE ** STEP) / (jnp.sqrt(second_new / (1.0 - BETA_TWO ** STEP)) + ADAM_EPS)
    return (first_new, second_new, weight_full - rate_value * (ratio + decay_rate * weight_full))

def reference(tokens, cotangent, routes, qkv_weight, out_weight, norm_gain, bias_rows, router_weight, expand_weight, shrink_weight, expert_bias, first_qkv, first_out, first_gain, first_bias, first_router, first_expand, first_shrink, first_expert, second_qkv, second_out, second_gain, second_bias, second_router, second_expand, second_shrink, second_expert):
    weights_all = (qkv_weight, out_weight, norm_gain, bias_rows, router_weight, expand_weight, shrink_weight, expert_bias)
    params = tuple([weight.astype(jnp.float32) for weight in weights_all])
    model_width = tokens.shape[2]
    images_all = tokens.shape[0] * tokens.shape[1] // SEQ
    group_size = math.gcd(images_all, 16)
    inputs = tokens.astype(jnp.float32).reshape(images_all // group_size, group_size, SEQ, model_width)
    route_groups = routes.reshape(images_all // group_size, group_size, SEQ, routes.shape[2])

    def forward(params, inputs):

        def one_group(running, group_item):
            return (running, jax.checkpoint(block)(params, group_item[0], group_item[1]))
        _, outputs = lax.scan(one_group, jnp.zeros((), jnp.float32), (inputs, route_groups))
        return outputs
    outputs, pullback = jax.vjp(forward, params, inputs)
    param_grads, input_grads = pullback(cotangent.reshape(outputs.shape))
    firsts = (first_qkv, first_out, first_gain, first_bias, first_router, first_expand, first_shrink, first_expert)
    seconds = (second_qkv, second_out, second_gain, second_bias, second_router, second_expand, second_shrink, second_expert)
    updates = [adam_update(weights_all[kind_index], param_grads[kind_index], firsts[kind_index], seconds[kind_index], RATES[kind_index], DECAYS[kind_index]) for kind_index in range(8)]
    output = outputs.reshape(tokens.shape)
    input_grad = input_grads.reshape(tokens.shape)
    return (output, input_grad, updates[0][0], updates[0][1], updates[0][2], updates[1][0], updates[1][1], updates[1][2], updates[2][0], updates[2][1], updates[2][2], updates[3][0], updates[3][1], updates[3][2], updates[4][0], updates[4][1], updates[4][2], updates[5][0], updates[5][1], updates[5][2], updates[6][0], updates[6][1], updates[6][2], updates[7][0], updates[7][1], updates[7][2])
```

```python
import jax
import jax.numpy as jnp
from jax import lax
from jax.experimental import pallas as pl
from jax.experimental.pallas import tpu as pltpu
from jax.sharding import Mesh
from jax.sharding import PartitionSpec as P

HEAD = 64
SEQ = 197
STEP = 10
CAP = 133
CHIPS = ("dev_0", "dev_1", "dev_2")
CORE = "dev_3"
DEV = ("dev_0", "dev_1", "dev_2", "dev_3")


NORM_EPS = 1e-06
ADAM_EPS = 1e-08
BETA_ONE = 0.9
BETA_TWO = 0.95
ROOT_HALF = 0.7071067811865476
INV_ROOT_TAU = 0.3989422804014327
RATES = (0.04, 0.2, 0.4, 0.04, 0.03, 0.04, 0.05, 0.04)
DECAYS = (0.1, 0.1, 0.0, 0.0, 0.1, 0.1, 0.1, 0.0)


def norm_parts(values):
    average = jnp.mean(values, -1, keepdims=True)
    centred = values - average
    inverse = lax.rsqrt(jnp.mean(centred * centred, -1, keepdims=True) + NORM_EPS)
    return (centred * inverse, inverse)


def norm_back(grad_norm, normed, inverse):
    return inverse * (
        grad_norm
        - jnp.mean(grad_norm, -1, keepdims=True)
        - normed * jnp.mean(grad_norm * normed, -1, keepdims=True)
    )


def softmax_rows(logits):
    shifted = jnp.exp(logits - jnp.max(logits, -1, keepdims=True))
    return shifted / jnp.sum(shifted, -1, keepdims=True)


def swap_cores(x):
    return lax.ppermute(x, CORE, [(0, 1), (1, 0)])


def pad_rows(x, length):
    return jnp.pad(x, [(0, 0)] * (x.ndim - 2) + [(0, length - x.shape[-2]), (0, 0)])


def smalls_by_row(gain, bias, router, ebias):
    rows = router.shape[0]
    turned = ebias.reshape(3, rows // 6, 5, 6).transpose(1, 3, 0, 2).reshape(rows, 15)
    return jnp.concatenate([gain.T, bias.T, router, turned], axis=1)


def smalls_apart(x):
    rows = x.shape[0]
    ebias = x[:, 10:25].reshape(rows // 6, 6, 3, 5).transpose(2, 0, 3, 1).reshape(3, -1)
    return x[:, :2].T, x[:, 2:7].T, x[:, 7:10], ebias


def ring_sum(x, place, name):
    me = lax.axis_index(name)
    sign = 1 - 2 * lax.axis_index(CORE)
    perm = [(2 * i, 2 * ((i + 1) % 4)) for i in range(4)]
    perm += [(2 * i + 1, 2 * ((i - 1) % 4) + 1) for i in range(4)]
    moving = None
    for step in range(4):
        index = lax.rem(me - sign * (1 + step) + 8, 4)
        piece = lax.dynamic_index_in_dim(x, index, place, keepdims=False)
        if moving is not None:
            piece = moving.astype(jnp.float32) + piece.astype(jnp.float32)
        if step == 3:
            return piece
        moving = lax.ppermute(piece.astype(jnp.bfloat16), (name, CORE), perm)


def sum_over_chips(x, first):
    names = list(CHIPS)
    x = ring_sum(x, first, names.pop(first)).astype(jnp.bfloat16)
    second = first % 2
    x = ring_sum(x, second, names.pop(second)).astype(jnp.bfloat16)
    return ring_sum(x, 0, names[0])


def gelu_both(z):
    half = 0.5 * (1.0 + lax.erf(z * ROOT_HALF))
    return z * half, half + z * jnp.exp(-0.5 * z * z) * INV_ROOT_TAU


SLOTS = 272


def mm(a, b, dims):
    return lax.dot_general(a, b, (dims, ((), ())), preferred_element_type=jnp.float32)


def two_terms(x):
    high = x.astype(jnp.bfloat16)
    return high, (x - high.astype(jnp.float32)).astype(jnp.bfloat16)


def expert_kernel(
    core_ref, w2_ref, w1_ref, b1_ref, b2_ref, x_ref, cot_ref, slot_row_ref, slot_col_ref, gate_ref,
    out_in_ref, dx_in_ref,
    own1_ref, send1_ref, own2_ref, send2_ref, db1_ref, db2_ref, out_ref, dx_ref, gg_ref,
    xs, xts, rs, rows_acc, dx_acc,
):
    i = pl.program_id(0)
    core = core_ref[0]
    tokens = x_ref.shape[0]

    @pl.when(i == 0)
    def _():
        pick = (
            lax.broadcasted_iota(jnp.int32, (SLOTS, tokens), 0) == slot_row_ref[...]
        ).astype(jnp.float32).astype(jnp.bfloat16)
        taken = mm(pick, x_ref[...], ((1,), (0,)))
        xs[...] = taken.astype(jnp.bfloat16)
        xts[...] = taken.T.astype(jnp.bfloat16)
        grads = mm(pick, (gate_ref[...] * cot_ref[...]).astype(jnp.bfloat16), ((1,), (0,)))
        rs[...] = grads.astype(jnp.bfloat16)
        db2_ref[...] = jnp.sum(grads, 0, keepdims=True)
        rows_acc[...] = jnp.zeros_like(rows_acc) + b2_ref[...]
        dx_acc[...] = jnp.zeros_like(dx_acc)

    x = xs[...]
    r = rs[...]
    w1 = w1_ref[...].astype(jnp.float32).reshape(1024, 768).astype(jnp.bfloat16)
    w2 = w2_ref[...].astype(jnp.float32).reshape(768, 768).astype(jnp.bfloat16)
    hidden = mm(x, w1, ((1,), (0,))) + b1_ref[...]
    act, slope = gelu_both(hidden)
    act = act.astype(jnp.bfloat16)
    rows_acc[...] += mm(act, w2, ((1,), (0,)))
    dw2 = mm(act, r, ((0,), (0,))).reshape(16, 2, 3, 8, 768)
    own2_ref[...] = jnp.where(core == 0, dw2[:, 0], dw2[:, 1]).astype(jnp.bfloat16)
    send2_ref[...] = jnp.where(core == 0, dw2[:, 1], dw2[:, 0]).astype(jnp.bfloat16)
    dh = mm(r, w2, ((1,), (1,))) * slope
    dh = dh.astype(jnp.bfloat16)
    db1_ref[...] = jnp.sum(dh.astype(jnp.float32), 0, keepdims=True)
    dw1 = mm(xts[...], dh, ((1,), (0,))).reshape(64, 2, 1, 8, 768)
    own1_ref[...] = jnp.where(core == 0, dw1[:, 0], dw1[:, 1]).astype(jnp.bfloat16)
    send1_ref[...] = jnp.where(core == 0, dw1[:, 1], dw1[:, 0]).astype(jnp.bfloat16)
    dx_acc[...] += mm(dh, w1, ((1,), (1,)))

    @pl.when(i == pl.num_programs(0) - 1)
    def _():
        put = (
            lax.broadcasted_iota(jnp.int32, (tokens, SLOTS), 1) == slot_col_ref[...]
        ).astype(jnp.float32).astype(jnp.bfloat16)
        high, low = two_terms(rows_acc[...])
        rows = mm(put, high, ((1,), (0,))) + mm(put, low, ((1,), (0,)))
        out_ref[...] = out_in_ref[...] + gate_ref[...] * rows
        gg_ref[...] = jnp.sum(rows * cot_ref[...], 1, keepdims=True)
        high, low = two_terms(dx_acc[...])
        dx_ref[...] = dx_in_ref[...] + (mm(put, high, ((1,), (0,))) + mm(put, low, ((1,), (0,))))


def run_expert(e, core, whole, b1, b2, x, cot, slot_row, slot_col, gate, out_in, dx_in):
    tokens = x.shape[0]
    bf, f32 = jnp.bfloat16, jnp.float32

    def all_of(shape):
        return pl.BlockSpec(shape, lambda i: (0,) * len(shape))

    return pl.pallas_call(
        expert_kernel,
        grid=(4,),
        in_specs=[
            pl.BlockSpec(memory_space=pltpu.SMEM),
            pl.BlockSpec((32, None, 3, 8, 768), lambda i: (i, e, 0, 0, 0)),
            pl.BlockSpec((128, None, 1, 8, 768), lambda i: (0, e, 3 + i, 0, 0)),
            pl.BlockSpec((1, 768), lambda i: (0, i)),
            all_of((1, 768)),
            all_of((tokens, 1024)),
            all_of((tokens, 768)),
            all_of((1, tokens)),
            all_of((tokens, 1)),
            all_of((tokens, 1)),
            all_of((tokens, 768)),
            all_of((tokens, 1024)),
        ],
        out_specs=[
            pl.BlockSpec((64, 1, 8, 768), lambda i: (0, i, 0, 0)),
            pl.BlockSpec((64, 1, 8, 768), lambda i: (0, i, 0, 0)),
            pl.BlockSpec((16, 3, 8, 768), lambda i: (i, 0, 0, 0)),
            pl.BlockSpec((16, 3, 8, 768), lambda i: (i, 0, 0, 0)),
            pl.BlockSpec((1, 768), lambda i: (0, i)),
            all_of((1, 768)),
            all_of((tokens, 768)),
            all_of((tokens, 1024)),
            all_of((tokens, 1)),
        ],
        out_shape=[
            jax.ShapeDtypeStruct((64, 4, 8, 768), bf),
            jax.ShapeDtypeStruct((64, 4, 8, 768), bf),
            jax.ShapeDtypeStruct((64, 3, 8, 768), bf),
            jax.ShapeDtypeStruct((64, 3, 8, 768), bf),
            jax.ShapeDtypeStruct((1, 3072), f32),
            jax.ShapeDtypeStruct((1, 768), f32),
            jax.ShapeDtypeStruct((tokens, 768), f32),
            jax.ShapeDtypeStruct((tokens, 1024), f32),
            jax.ShapeDtypeStruct((tokens, 1), f32),
        ],
        scratch_shapes=[
            pltpu.VMEM((SLOTS, 1024), bf),
            pltpu.VMEM((1024, SLOTS), bf),
            pltpu.VMEM((SLOTS, 768), bf),
            pltpu.VMEM((SLOTS, 768), f32),
            pltpu.VMEM((SLOTS, 1024), f32),
        ],
        compiler_params=pltpu.CompilerParams(vmem_limit_bytes=58 * 1024 * 1024),
        cost_estimate=pl.CostEstimate(
            flops=6 * 2 * SLOTS * 900 * 3072, bytes_accessed=30_000_000, transcendentals=2_000_000
        ),
    )(core, whole, whole, b1, b2, x, cot, slot_row, slot_col, gate, out_in, dx_in)


def adam_update(weight, gradient, first_old, second_old, rate_value, decay_rate):
    first_new = BETA_ONE * first_old + (1.0 - BETA_ONE) * gradient
    second_new = BETA_TWO * second_old + (1.0 - BETA_TWO) * gradient * gradient
    weight_full = weight.astype(jnp.float32)
    ratio = (
        first_new
        / (1.0 - BETA_ONE**STEP)
        / (jnp.sqrt(second_new / (1.0 - BETA_TWO**STEP)) + ADAM_EPS)
    )
    return (first_new, second_new, weight_full - rate_value * (ratio + decay_rate * weight_full))


def dot(a, b):
    return jnp.dot(a, b, preferred_element_type=jnp.float32)


def ein(spec, a, b):
    return jnp.einsum(spec, a, b, preferred_element_type=jnp.float32)


def on_device(
    tokens,
    cotangent,
    routes,
    qkv_weight,
    out_weight,
    norm_gain,
    bias_rows,
    router_weight,
    expand_weight,
    shrink_weight,
    expert_bias,
    *moments,
):
    f32, bf = jnp.float32, jnp.bfloat16
    core = lax.axis_index(CORE)
    micro, rows_each, width = tokens.shape
    count = micro * rows_each
    heads = width // HEAD
    scaling = HEAD ** (-0.5)

    attn_own = jnp.concatenate(
        [qkv_weight, out_weight, smalls_by_row(norm_gain, bias_rows, router_weight, expert_bias)], 1
    )
    attn_own = jnp.pad(attn_own, [(0, 2), (0, 103)])
    mine = lax.all_to_all(jnp.broadcast_to(attn_own, (64, 8, 3200)), CHIPS, 0, 0, tiled=True)
    other = swap_cores(mine)
    attn_whole = jnp.where(
        core == 0, jnp.stack([mine, other], 1), jnp.stack([other, mine], 1)
    )
    attn_whole = attn_whole[:, :, :6].reshape(width, 3200)

    w1_own = pad_rows(expand_weight, 8).reshape(3, 8, 4, 768).transpose(0, 2, 1, 3)
    expert_own = jnp.concatenate([shrink_weight.reshape(3, 3, 8, 768), w1_own], 1)
    expert_whole = lax.all_gather(expert_own[None], DEV, axis=0, tiled=True)

    qkv_full = attn_whole[:, :2304]
    out_full = attn_whole[:, 2304:3072]
    gain_full, shift_full, router_full, ebias_full = smalls_apart(attn_whole[:, 3072:])
    gains = gain_full.astype(f32)
    shifts = shift_full.astype(f32)
    ebias = ebias_full.astype(f32)

    route_rows = routes.reshape(count, 2)
    hot = (route_rows[:, :, None] == jnp.arange(3, dtype=jnp.int32)).astype(f32)
    member = jnp.sum(hot, 1)
    lower = (jnp.arange(count)[:, None] >= jnp.arange(count)[None, :]).astype(bf)
    position = (dot(lower, member.astype(bf)) - 1.0).astype(jnp.int32)
    slots = jnp.where(member > 0, position, -1)

    spread = (
        (jnp.arange(width) // 6 * 8 + jnp.arange(width) % 6)[:, None] == jnp.arange(1024)[None, :]
    ).astype(bf)

    residual = tokens.reshape(count, width).astype(f32)
    normed_one, inverse_one = norm_parts(residual)
    attn_input = (normed_one * gains[0] + shifts[0]).astype(bf)
    attn_input_wide = dot(attn_input, spread).astype(bf)
    qkv_bias = jnp.concatenate([shifts[2], jnp.zeros_like(shifts[2]), shifts[3]])
    qkv_rows = (dot(attn_input, qkv_full) + qkv_bias).astype(bf)
    split_rows = qkv_rows.reshape(micro, SEQ, 3, heads, HEAD)
    queries, keys, values = split_rows[:, :, 0], split_rows[:, :, 1], split_rows[:, :, 2]
    scores = ein("iqhc,ikhc->ihqk", queries, keys) * scaling
    probs = softmax_rows(scores)
    weights = probs.astype(bf)
    attended = ein("ihqk,ikhc->iqhc", weights, values).reshape(count, width).astype(bf)
    attended_wide = dot(attended, spread).astype(bf)
    middle = residual + dot(attended, out_full) + shifts[4]
    normed_two, inverse_two = norm_parts(middle)
    expert_input = (normed_two * gains[1] + shifts[1]).astype(bf)
    expert_input_wide = dot(expert_input, spread).astype(bf)
    router_prob = softmax_rows(dot(expert_input, router_full))
    picked = jnp.sum(hot * router_prob[:, None, :], -1)
    picked_sum = jnp.sum(picked, -1, keepdims=True)
    gate_share = picked / picked_sum
    gate_by_expert = jnp.sum(hot * gate_share[:, :, None], 1)

    grad_out = cotangent.reshape(count, width)
    output = middle
    wide_grad = jnp.zeros((count, 1024), f32)
    core_word = core.astype(jnp.int32).reshape(1)
    gate_grads, inner, outer, sums = [], [], [], []
    for e in range(3):
        own1, send1, own2, send2, db1, db2, output, wide_grad, gg = run_expert(
            e, core_word, expert_whole, ebias[e : e + 1, :3072], ebias[e : e + 1, 3072:],
            expert_input_wide, grad_out, slots[:, e].reshape(1, count), slots[:, e : e + 1],
            gate_by_expert[:, e : e + 1], output, wide_grad,
        )
        gate_grads.append(gg)
        inner.append(db1)
        outer.append(db2)
        pair = jnp.concatenate(
            [
                own1.astype(f32) + swap_cores(send1).astype(f32),
                own2.astype(f32) + swap_cores(send2).astype(f32),
            ],
            1,
        ).astype(bf)
        sums.append(sum_over_chips(pair.reshape(4, 4, 4, 7, 8, 768), e))

    gate_grad = jnp.sum(hot * jnp.concatenate(gate_grads, 1)[:, None, :], -1)
    picked_grad = (gate_grad - jnp.sum(gate_grad * gate_share, -1, keepdims=True)) / picked_sum
    prob_grad = jnp.sum(hot * picked_grad[:, :, None], 1)
    logit_grad = (
        router_prob * (prob_grad - jnp.sum(router_prob * prob_grad, -1, keepdims=True))
    ).astype(bf)
    router_grad = ein("td,te->de", expert_input, logit_grad)
    high, low = two_terms(wide_grad)
    input_two_grad = (
        ein("tw,dw->td", high, spread)
        + ein("tw,dw->td", low, spread)
        + ein("te,de->td", logit_grad, router_full)
    )
    gain_two_grad = jnp.sum(input_two_grad * normed_two, 0)
    shift_two_grad = jnp.sum(input_two_grad, 0)
    middle_grad = grad_out + norm_back(input_two_grad * gains[1], normed_two, inverse_two)

    branch_grad = middle_grad.astype(bf)
    out_grad = ein("td,te->de", attended_wide, branch_grad)
    out_bias_grad = jnp.sum(branch_grad, 0, dtype=f32)
    attended_grad = ein("te,de->td", branch_grad, out_full).astype(bf)
    attended_grad = attended_grad.reshape(micro, SEQ, heads, HEAD)
    value_grad = ein("ihqk,iqhc->ikhc", weights, attended_grad)
    attn_prob_grad = ein("iqhc,ikhc->ihqk", attended_grad, values)
    score_grad = (
        probs * (attn_prob_grad - jnp.sum(probs * attn_prob_grad, -1, keepdims=True))
    ).astype(bf)
    query_grad = ein("ihqk,ikhc->iqhc", score_grad, keys) * scaling
    key_grad = ein("ihqk,iqhc->ikhc", score_grad, queries) * scaling
    qkv_grad = (
        jnp.stack([query_grad, key_grad, value_grad], 2).reshape(count, 3 * width).astype(bf)
    )
    qkv_weight_grad = ein("td,te->de", attn_input_wide, qkv_grad)
    qkv_bias_grad = jnp.sum(qkv_grad, 0, dtype=f32)
    input_one_grad = ein("te,de->td", qkv_grad, qkv_full)
    gain_one_grad = jnp.sum(input_one_grad * normed_one, 0)
    shift_one_grad = jnp.sum(input_one_grad, 0)
    input_grad = middle_grad + norm_back(input_one_grad * gains[0], normed_one, inverse_one)

    small_grads = smalls_by_row(
        jnp.stack([gain_one_grad, gain_two_grad]),
        jnp.stack(
            [
                shift_one_grad,
                shift_two_grad,
                qkv_bias_grad[:width],
                qkv_bias_grad[2 * width :],
                out_bias_grad,
            ]
        ),
        router_grad,
        jnp.concatenate([jnp.concatenate(inner, 0), jnp.concatenate(outer, 0)], 1),
    )
    small_grads = jnp.pad(small_grads.reshape(128, 6, 25), [(0, 0), (0, 2), (0, 103)])
    attn_grads = jnp.concatenate(
        [qkv_weight_grad, out_grad, small_grads.reshape(1024, 128)], 1
    ).astype(bf).reshape(64, 2, 8, 3200)
    keep = lax.dynamic_index_in_dim(attn_grads, core, 1, keepdims=False)
    give = lax.dynamic_index_in_dim(attn_grads, 1 - core, 1, keepdims=False)
    pair = (keep.astype(f32) + swap_cores(give).astype(f32)).astype(bf)
    attn_sum = lax.all_to_all(pair, CHIPS, 0, 0, tiled=True)
    attn_sum = jnp.sum(attn_sum.astype(f32), 0)[:6]
    gain_sum, shift_sum, router_sum, ebias_sum = smalls_apart(attn_sum[:, 3072:])
    expert_sums = jnp.stack(sums)
    expand_sum = expert_sums[:, :4, :6].transpose(0, 2, 1, 3).reshape(3, 6, 3072)
    shrink_sum = expert_sums[:, 4:].reshape(3, 24, 768)

    weights_all = (
        qkv_weight,
        out_weight,
        norm_gain,
        bias_rows,
        router_weight,
        expand_weight,
        shrink_weight,
        expert_bias,
    )
    grads_all = (
        attn_sum[:, :2304],
        attn_sum[:, 2304:3072],
        gain_sum,
        shift_sum,
        router_sum,
        expand_sum,
        shrink_sum,
        ebias_sum,
    )
    results = [output.reshape(tokens.shape), input_grad.reshape(tokens.shape)]
    for k in range(8):
        results.extend(
            adam_update(
                weights_all[k], grads_all[k], moments[k], moments[8 + k], RATES[k], DECAYS[k]
            )
        )
    return tuple(results)


def solution(mesh):
    split = Mesh(mesh.devices.reshape(4, 4, 4, 2), ("dev_0", "dev_1", "dev_2", "dev_3"))
    placed = (
        P(None, DEV, None),
        P(None, DEV, None),
        P(None, DEV, None),
        P(DEV, None),
        P(DEV, None),
        P(None, DEV),
        P(None, DEV),
        P(DEV, None),
        P(None, DEV, None),
        P(None, DEV, None),
        P(None, DEV),
        P(DEV, None),
        P(DEV, None),
        P(None, DEV),
        P(None, DEV),
        P(DEV, None),
        P(None, DEV, None),
        P(None, DEV, None),
        P(None, DEV),
        P(DEV, None),
        P(DEV, None),
        P(None, DEV),
        P(None, DEV),
        P(DEV, None),
        P(None, DEV, None),
        P(None, DEV, None),
        P(None, DEV),
    )
    return jax.shard_map(
        on_device,
        mesh=split,
        in_specs=placed,
        out_specs=(
            P(None, DEV, None),
            P(None, DEV, None),
            P(DEV, None),
            P(DEV, None),
            P(DEV, None),
            P(DEV, None),
            P(DEV, None),
            P(DEV, None),
            P(None, DEV),
            P(None, DEV),
            P(None, DEV),
            P(None, DEV),
            P(None, DEV),
            P(None, DEV),
            P(DEV, None),
            P(DEV, None),
            P(DEV, None),
            P(None, DEV, None),
            P(None, DEV, None),
            P(None, DEV, None),
            P(None, DEV, None),
            P(None, DEV, None),
            P(None, DEV, None),
            P(None, DEV),
            P(None, DEV),
            P(None, DEV),
        ),
        check_vma=False,
    )
```

```python
import functools

import jax
import jax.numpy as jnp
from jax import lax
from jax.experimental import pallas as pl
from jax.experimental.pallas import tpu as pltpu
from jax.sharding import Mesh
from jax.sharding import PartitionSpec as P

HEAD = 64
SEQ = 197
STEP = 10
CAP = 133
CHIPS = ("dev_0", "dev_1", "dev_2")
CORE = "dev_3"
DEV = ("dev_0", "dev_1", "dev_2", "dev_3")


NORM_EPS = 1e-06
ADAM_EPS = 1e-08
BETA_ONE = 0.9
BETA_TWO = 0.95
ROOT_HALF = 0.7071067811865476
INV_ROOT_TAU = 0.3989422804014327
RATES = (0.04, 0.2, 0.4, 0.04, 0.03, 0.04, 0.05, 0.04)
DECAYS = (0.1, 0.1, 0.0, 0.0, 0.1, 0.1, 0.1, 0.0)


def norm_parts(values):
    average = jnp.mean(values, -1, keepdims=True)
    centred = values - average
    inverse = lax.rsqrt(jnp.mean(centred * centred, -1, keepdims=True) + NORM_EPS)
    return (centred * inverse, inverse)


def norm_back(grad_norm, normed, inverse):
    return inverse * (
        grad_norm
        - jnp.mean(grad_norm, -1, keepdims=True)
        - normed * jnp.mean(grad_norm * normed, -1, keepdims=True)
    )


def softmax_rows(logits):
    shifted = jnp.exp(logits - jnp.max(logits, -1, keepdims=True))
    return shifted / jnp.sum(shifted, -1, keepdims=True)


def swap_cores(x):
    return lax.ppermute(x, CORE, [(0, 1), (1, 0)])


def pad_rows(x, length):
    return jnp.pad(x, [(0, 0)] * (x.ndim - 2) + [(0, length - x.shape[-2]), (0, 0)])


def ring_pairs():
    up = [(2 * i, 2 * ((i + 1) % 4)) for i in range(4)]
    return up + [(2 * i + 1, 2 * ((i - 1) % 4) + 1) for i in range(4)]


def chips_gather(x):
    sign = 1 - 2 * lax.axis_index(CORE)
    moving = lax.all_to_all(jnp.broadcast_to(x, (16, *x.shape)), CHIPS[1:], 0, 0, tiled=True)
    whole = jnp.zeros((4, *moving.shape), x.dtype)
    for step in range(4):
        index = lax.rem(lax.axis_index(CHIPS[0]) - sign * step + 4, 4)
        whole = lax.dynamic_update_index_in_dim(whole, moving, index, 0)
        if step < 3:
            moving = lax.ppermute(moving, (CHIPS[0], CORE), ring_pairs())
    return whole


def round_kernel(sizes, carried, index_ref, *refs):
    outs = refs[len(refs) - carried - len(sizes) : len(refs) - carried]
    at = 0
    for size, out_ref in zip(sizes, outs):
        total = sum([refs[at + k][...].astype(jnp.float32) for k in range(size)])
        out_ref[...] = total.astype(jnp.bfloat16)
        at += size


class Ring:
    def __init__(self, own, received, place):
        self.shape = own.shape[1:]
        self.terms = [a.reshape(4, 4, 4, *self.shape) for a in (own, received)]
        self.place, self.name = place, CHIPS[place]
        self.plane = tuple([c for c in CHIPS if c != self.name])
        self.step, self.piece = 0, None

    def pass_on(self):
        return lax.ppermute(self.piece, (self.name, CORE), ring_pairs())

    def total(self):
        blocks = self.piece.reshape(16, *self.shape)
        blocks = lax.all_to_all(blocks, self.plane, 0, 0, tiled=True)
        return jnp.sum(blocks.astype(jnp.float32), 0)


def next_round(rings, after=(), carry=()):
    sign = 1 - 2 * lax.axis_index(CORE)
    index, arrays, specs, sizes = [], [], [], []
    outs = []
    for n, ring in enumerate(rings):
        index.append(lax.rem(lax.axis_index(ring.name) - sign * (1 + ring.step) + 8, 4))
        block = [1, 4]
        block.insert(ring.place, None)
        tail = (0,) * len(ring.shape)

        def where(g, index_ref, place=ring.place, n=n, tail=tail):
            at = [g, 0]
            at.insert(place, index_ref[n])
            return (*at, *tail)

        moved = pl.BlockSpec((1, 4, *ring.shape), lambda g, _, tail=tail: (g, 0, *tail))
        arrays += ring.terms
        specs += [pl.BlockSpec((*block, *ring.shape), where)] * 2
        if ring.step:
            arrays.append(ring.pass_on())
            specs.append(moved)
        sizes.append(3 if ring.step else 2)
        outs.append((jax.ShapeDtypeStruct((4, 4, *ring.shape), jnp.bfloat16), moved))
    at = 1 + len(arrays) + len(after)
    *pieces, = pl.pallas_call(
        functools.partial(round_kernel, sizes, len(carry)),
        grid_spec=pltpu.PrefetchScalarGridSpec(
            num_scalar_prefetch=1,
            grid=(4,),
            in_specs=specs + [pl.BlockSpec(memory_space=pl.ANY)] * (len(after) + len(carry)),
            out_specs=[spec for _, spec in outs]
            + [pl.BlockSpec(memory_space=pl.ANY)] * len(carry),
        ),
        out_shape=[shape for shape, _ in outs]
        + [jax.ShapeDtypeStruct(a.shape, a.dtype) for a in carry],
        input_output_aliases={at + k: len(outs) + k for k in range(len(carry))},
        compiler_params=pltpu.CompilerParams(vmem_limit_bytes=58 * 1024 * 1024),
        cost_estimate=pl.CostEstimate(
            flops=0, bytes_accessed=5_500_000 * len(rings), transcendentals=0
        ),
    )(jnp.stack(index).astype(jnp.int32), *arrays, *after, *carry)
    for ring, piece in zip(rings, pieces):
        ring.step, ring.piece = ring.step + 1, piece
    return tuple(pieces)


def gelu_both(z):
    half = 0.5 * (1.0 + lax.erf(z * ROOT_HALF))
    return z * half, half + z * jnp.exp(-0.5 * z * z) * INV_ROOT_TAU


SLOTS = 272


def mm(a, b, dims):
    return lax.dot_general(a, b, (dims, ((), ())), preferred_element_type=jnp.float32)


def two_terms(x):
    high = x.astype(jnp.bfloat16)
    return high, (x - high.astype(jnp.float32)).astype(jnp.bfloat16)


def to_wide(core, mine, other):
    mine, other = mine.astype(jnp.float32), other.astype(jnp.float32)
    both = jnp.stack([jnp.where(core == 0, mine, other), jnp.where(core == 0, other, mine)], 1)
    return both.reshape(1024, both.shape[-1]).astype(jnp.bfloat16)


def by_core(core, x, own_ref, send_ref):
    parts = x.reshape(own_ref.shape[0], 2, *own_ref.shape[1:])
    own_ref[...] = jnp.where(core == 0, parts[:, 0], parts[:, 1]).astype(jnp.bfloat16)
    send_ref[...] = jnp.where(core == 0, parts[:, 1], parts[:, 0]).astype(jnp.bfloat16)


def spread_out(x, spread):
    return mm(x, spread, ((1,), (0,))).astype(jnp.bfloat16)


def pull_in(x, spread):
    high, low = two_terms(x)
    return mm(high, spread, ((1,), (1,))) + mm(low, spread, ((1,), (1,)))


def ones_where(mask):
    return mask.astype(jnp.float32).astype(jnp.bfloat16)


def biases_of_devices():
    device = lax.broadcasted_iota(jnp.int32, (128, 3840), 0)
    value = lax.broadcasted_iota(jnp.int32, (128, 3840), 1)
    return (value >= 30 * device) & (value < 30 * device + 30)


def spare_rows():
    place = lax.broadcasted_iota(jnp.int32, (1024, 128), 0)
    return ones_where(place == 8 * lax.broadcasted_iota(jnp.int32, (1024, 128), 1) + 6)


def qkv_kernel(
    core_ref, mine_ref, other_ref, small_mine_ref, small_other_ref, spread_ref, tokens_ref,
    of_device_ref, qkv_ref, wide_ref, small_ref, ebias_ref,
):
    j = pl.program_id(0)
    core = core_ref[0]

    @pl.when(j == 0)
    def _():
        small = to_wide(core, small_mine_ref[...], small_other_ref[...])
        small_ref[...] = mm(small, spread_ref[...], ((0,), (1,)))
        blocks = mm(spare_rows(), small, ((0,), (0,))).astype(jnp.bfloat16)
        for e in range(3):
            spaced = mm(blocks[:, 32 * e : 32 * e + 32], of_device_ref[:, :32], ((1,), (1,)))
            ebias_ref[e] = jnp.sum(jnp.where(biases_of_devices(), spaced, 0.0), 0, keepdims=True)
        for b in range(2):
            normed, _ = norm_parts(tokens_ref[b].astype(jnp.float32))
            rows = (normed * small_ref[0:1] + small_ref[2:3]).astype(jnp.bfloat16)
            wide_ref[b] = spread_out(rows, spread_ref[...])

    weight = to_wide(core, mine_ref[...], other_ref[...])
    bias = jnp.where(j == 0, small_ref[4:5], jnp.where(j == 1, 0.0, small_ref[5:6]))
    for b in range(2):
        qkv_ref[b] = (mm(wide_ref[b], weight, ((1,), (0,))) + bias).astype(jnp.bfloat16)


def head_probs(query, key):
    scores = mm(query, key, ((1,), (1,))) * (HEAD ** (-0.5))
    return softmax_rows(scores)


def attend_kernel(
    core_ref, mine_ref, other_ref, qkv_ref, tokens_ref, routes_ref, small_ref, spread_ref,
    attended_ref, middle_ref, input_ref, prob_ref, gate_ref, kept,
):
    core = core_ref[0]
    width = tokens_ref.shape[-1]
    for pair in range(width // (2 * HEAD)):
        parts = []
        for h in (2 * pair, 2 * pair + 1):
            query, key, value = [
                qkv_ref[:, k * width + h * HEAD : k * width + (h + 1) * HEAD] for k in range(3)
            ]
            weights = head_probs(query, key).astype(jnp.bfloat16)
            parts.append(mm(weights, value, ((1,), (0,))))
        kept[:, pair * 128 : pair * 128 + 128] = jnp.concatenate(parts, 1).astype(jnp.bfloat16)
    spread = spread_ref[...]
    attended = spread_out(kept[...], spread)
    attended_ref[...] = attended
    weight = to_wide(core, mine_ref[...], other_ref[...])
    branch = mm(attended, weight, ((1,), (0,))) + small_ref[6:7]
    middle = tokens_ref[...].astype(jnp.float32) + branch
    middle_ref[...] = middle
    normed, _ = norm_parts(middle)
    rows = (normed * small_ref[1:2] + small_ref[3:4]).astype(jnp.bfloat16)
    input_ref[...] = spread_out(rows, spread)
    logits = mm(rows, small_ref[7:10].astype(jnp.bfloat16), ((1,), (1,)))
    prob = softmax_rows(logits)
    prob_ref[...] = prob
    experts = lax.broadcasted_iota(jnp.int32, prob.shape, 1)
    routes = routes_ref[...]
    member = ((experts == routes[:, 0:1]) | (experts == routes[:, 1:2])).astype(jnp.float32)
    chosen = member * prob
    gate_ref[...] = chosen / jnp.sum(chosen, 1, keepdims=True)


def expert_kernel(
    e, core_ref, w2_ref, w1_ref, b1_ref, b2_ref, x_ref, cot_ref, slot_row_ref, slot_col_ref,
    gate_ref, out_in_ref, *rest,
):
    (
        own_ref, send_ref, db1_ref, db2_ref, out_ref, dx_ref, gg_ref,
        xs, xts, rs, rows_acc, dx_acc, kept, sems,
    ) = rest[-14:]
    dx_in_ref = rest[0] if e > 0 else None
    i = pl.program_id(0)
    core = core_ref[0]
    tokens = x_ref.shape[1]

    @pl.when(i == 0)
    def _():
        taken, grads = 0.0, 0.0
        for b in range(2):
            slots = lax.broadcasted_iota(jnp.int32, (SLOTS, tokens), 0)
            pick = ones_where(slots == slot_row_ref[b, e : e + 1, :])
            taken += mm(pick, x_ref[b], ((1,), (0,)))
            scaled = (gate_ref[b][:, e : e + 1] * cot_ref[b]).astype(jnp.bfloat16)
            grads += mm(pick, scaled, ((1,), (0,)))
        xs[...] = taken.astype(jnp.bfloat16)
        xts[...] = taken.T.astype(jnp.bfloat16)
        rs[...] = grads.astype(jnp.bfloat16)
        db2_ref[...] = jnp.sum(grads, 0, keepdims=True)
        rows_acc[...] = jnp.zeros_like(rows_acc) + b2_ref[...]
        dx_acc[...] = jnp.zeros_like(dx_acc)

    x = xs[...]
    r = rs[...]
    w1 = w1_ref[...].astype(jnp.float32).reshape(1024, 768).astype(jnp.bfloat16)
    w2 = w2_ref[...].astype(jnp.float32).reshape(768, 768).astype(jnp.bfloat16)
    hidden = mm(x, w1, ((1,), (0,))) + b1_ref[...]
    act, slope = gelu_both(hidden)
    act = act.astype(jnp.bfloat16)
    rows_acc[...] += mm(act, w2, ((1,), (0,)))
    dw2 = mm(act, r, ((0,), (0,))).reshape(16, 2, 3, 8, 768)
    for c in range(2):
        kept[c, pl.ds(pl.multiple_of(16 * i, 16), 16), 4:7] = dw2[:, c].astype(jnp.bfloat16)
    dh = mm(r, w2, ((1,), (1,))) * slope
    dh = dh.astype(jnp.bfloat16)
    db1_ref[...] = jnp.sum(dh.astype(jnp.float32), 0, keepdims=True)
    dw1 = mm(xts[...], dh, ((1,), (0,))).reshape(64, 2, 1, 8, 768)
    for c in range(2):
        kept[c, :, pl.ds(i, 1)] = dw1[:, c].astype(jnp.bfloat16)
    dx_acc[...] += mm(dh, w1, ((1,), (1,)))

    def copies(step):
        parts = [
            (slice(None), pl.ds(step, 1)),
            (pl.ds(pl.multiple_of(16 * step, 16), 16), pl.ds(4, 3)),
        ]
        pairs = [(kept.at[core], own_ref), (kept.at[1 - core], send_ref)]
        return [
            pltpu.make_async_copy(source.at[part], ref.at[part], sems.at[step, 2 * k + m])
            for k, (source, ref) in enumerate(pairs)
            for m, part in enumerate(parts)
        ]

    for copy in copies(i):
        copy.start()

    @pl.when(i == pl.num_programs(0) - 1)
    def _():
        rows_terms = two_terms(rows_acc[...])
        dx_terms = two_terms(dx_acc[...])
        for b in range(2):
            slots = lax.broadcasted_iota(jnp.int32, (tokens, SLOTS), 1)
            put = ones_where(slots == slot_col_ref[b][:, e : e + 1])
            rows = sum([mm(put, term, ((1,), (0,))) for term in rows_terms])
            out_ref[b] = out_in_ref[b] + gate_ref[b][:, e : e + 1] * rows
            gg_ref[b] = jnp.sum(rows * cot_ref[b], 1, keepdims=True)
            grad = sum([mm(put, term, ((1,), (0,))) for term in dx_terms])
            dx_ref[b] = grad if e == 0 else dx_in_ref[b] + grad
        for step in range(4):
            for copy in copies(step):
                copy.wait()


def route_back_kernel(
    core_ref, mine_ref, other_ref, dx_ref, gg0_ref, gg1_ref, gg2_ref, prob_ref, gate_ref,
    slots_ref, middle_ref, cot_ref, attended_ref, small_ref, spread_ref, *rest,
):
    grad_ref, attended_grad_ref, own_ref, send_ref, small_out_ref = rest[-5:]
    core = core_ref[0]
    spread = spread_ref[...]
    weight = to_wide(core, mine_ref[...], other_ref[...])
    router = small_ref[7:10].astype(jnp.bfloat16)
    total, sums, router_grad = 0.0, [0.0, 0.0, 0.0], 0.0
    for b in range(2):
        prob, gate = prob_ref[b], gate_ref[b]
        experts = lax.broadcasted_iota(jnp.int32, prob.shape, 1)
        gate_grad = jnp.where(
            experts == 0, gg0_ref[b], jnp.where(experts == 1, gg1_ref[b], gg2_ref[b])
        )
        member = (slots_ref[b] >= 0).astype(jnp.float32)
        chosen = jnp.sum(member * prob, 1, keepdims=True)
        share = jnp.sum(gate_grad * gate, 1, keepdims=True)
        prob_grad = member * (gate_grad - share) / chosen
        logit_grad = prob * (prob_grad - jnp.sum(prob * prob_grad, 1, keepdims=True))
        logit_grad = logit_grad.astype(jnp.bfloat16)
        normed, inverse = norm_parts(middle_ref[b])
        rows = (normed * small_ref[1:2] + small_ref[3:4]).astype(jnp.bfloat16)
        router_grad += mm(logit_grad, rows, ((0,), (0,)))
        grad = pull_in(dx_ref[b], spread) + mm(logit_grad, router, ((1,), (0,)))
        sums[0] += jnp.sum(grad * normed, 0, keepdims=True)
        sums[1] += jnp.sum(grad, 0, keepdims=True)
        grad = cot_ref[b] + norm_back(grad * small_ref[1:2], normed, inverse)
        grad_ref[b] = grad
        branch = grad.astype(jnp.bfloat16)
        sums[2] += jnp.sum(branch.astype(jnp.float32), 0, keepdims=True)
        total += mm(attended_ref[b], branch, ((0,), (0,)))
        wide = mm(branch, weight, ((1,), (1,))).astype(jnp.bfloat16)
        attended_grad_ref[b] = mm(wide, spread, ((1,), (1,))).astype(jnp.bfloat16)
    by_core(core, total, own_ref, send_ref)
    for k in range(3):
        small_out_ref[k : k + 1] = sums[k]
    small_out_ref[3:6] = router_grad


def attend_back_kernel(qkv_ref, grad_ref, *rest):
    out_ref = rest[-1]
    width = grad_ref.shape[-1]
    scaling = HEAD ** (-0.5)
    for pair in range(width // (2 * HEAD)):
        parts = [[], [], []]
        for h in (2 * pair, 2 * pair + 1):
            query, key, value = [
                qkv_ref[:, k * width + h * HEAD : k * width + (h + 1) * HEAD] for k in range(3)
            ]
            grad = grad_ref[:, h * HEAD : (h + 1) * HEAD]
            probs = head_probs(query, key)
            prob_grad = mm(grad, value, ((1,), (1,)))
            score_grad = probs * (prob_grad - jnp.sum(probs * prob_grad, 1, keepdims=True))
            score_grad = score_grad.astype(jnp.bfloat16)
            parts[0].append(mm(score_grad, key, ((1,), (0,))) * scaling)
            parts[1].append(mm(score_grad, query, ((0,), (0,))) * scaling)
            parts[2].append(mm(probs.astype(jnp.bfloat16), grad, ((0,), (0,))))
        for k in range(3):
            at = k * width + pair * 128
            out_ref[:, at : at + 128] = jnp.concatenate(parts[k], 1).astype(jnp.bfloat16)


def qkv_back_kernel(
    core_ref, mine_ref, other_ref, qkv_grad0_ref, qkv_grad1_ref, wide_ref, tokens_ref, grad_ref,
    small_ref, early_ref, in0_ref, in1_ref, in2_ref, out0_ref, out1_ref, out2_ref, of_device_ref,
    spread_ref, *rest,
):
    own_ref, send_ref, small_own_ref, small_send_ref, input_grad_ref, acc, sums = rest[-7:]
    j = pl.program_id(0)
    core = core_ref[0]
    weight = to_wide(core, mine_ref[...], other_ref[...])

    @pl.when(j == 0)
    def _():
        acc[...] = jnp.zeros_like(acc)
        sums[...] = jnp.zeros_like(sums)
        sums[1:2] = early_ref[0:1]
        sums[3:4] = early_ref[1:2]
        sums[6:10] = early_ref[2:6]

    total, bias = 0.0, 0.0
    for b in range(2):
        grad = (qkv_grad0_ref, qkv_grad1_ref)[b][...]
        total += mm(wide_ref[b], grad, ((0,), (0,)))
        bias += jnp.sum(grad.astype(jnp.float32), 0, keepdims=True)
        acc[b] += mm(grad, weight, ((1,), (1,)))
    by_core(core, total, own_ref, send_ref)

    @pl.when(j == 0)
    def _():
        sums[4:5] += bias

    @pl.when(j == 2)
    def _():
        sums[5:6] += bias
        spread = spread_ref[...]
        for b in range(2):
            normed, inverse = norm_parts(tokens_ref[b].astype(jnp.float32))
            grad = pull_in(acc[b], spread)
            sums[0:1] += jnp.sum(grad * normed, 0, keepdims=True)
            sums[2:3] += jnp.sum(grad, 0, keepdims=True)
            input_grad_ref[b] = grad_ref[b] + norm_back(grad * small_ref[0:1], normed, inverse)
        small = mm(spread, sums[...].astype(jnp.bfloat16), ((0,), (1,)))
        blocks = []
        for inner, outer in ((in0_ref, out0_ref), (in1_ref, out1_ref), (in2_ref, out2_ref)):
            biases = jnp.concatenate([inner[...], outer[...]], 1)
            spaced = jnp.where(biases_of_devices(), biases, 0.0).astype(jnp.bfloat16)
            blocks.append(mm(spaced, of_device_ref[...], ((1,), (0,)))[:, :32])
        blocks.append(jnp.zeros((128, 32), jnp.float32))
        blocks = jnp.concatenate(blocks, 1).astype(jnp.bfloat16)
        small += mm(spare_rows(), blocks, ((1,), (0,)))
        by_core(core, small, small_own_ref, small_send_ref)


def pair_kernel(own_qkv, got_qkv, own_out, got_out, own_small, got_small, *rest):
    out_ref = rest[-1]
    at = 0
    for own, got in ((own_qkv, got_qkv), (own_out, got_out), (own_small, got_small)):
        total = own[...].astype(jnp.float32) + got[...].astype(jnp.float32)
        out_ref[:, :, at : at + own.shape[2]] = total.astype(jnp.bfloat16)
        at += own.shape[2]


def sum_kernel(x_ref, *rest):
    rest[-1][...] = jnp.sum(x_ref[...].astype(jnp.float32), 0)


def call(kernel, grid, ins, outs, scratch=(), after=(), flops=0):
    def spec(shape, block, index):
        if block == "any":
            return pl.BlockSpec(memory_space=pl.ANY)
        if block is None:
            return pl.BlockSpec(shape, lambda *_: (0,) * len(shape))
        return pl.BlockSpec(block, index)

    in_specs = [
        pl.BlockSpec(memory_space=pltpu.SMEM)
        if block == "smem"
        else spec(array.shape, block, index)
        for array, block, index in ins
    ]
    in_specs += [pl.BlockSpec(memory_space=pl.ANY)] * len(after)
    arrays = [array for array, _, _ in ins]
    return pl.pallas_call(
        kernel,
        grid=grid,
        in_specs=in_specs,
        out_specs=[spec(shape, block, index) for shape, _, block, index in outs],
        out_shape=[jax.ShapeDtypeStruct(shape, kind) for shape, kind, _, _ in outs],
        scratch_shapes=list(scratch),
        compiler_params=pltpu.CompilerParams(vmem_limit_bytes=58 * 1024 * 1024),
        cost_estimate=pl.CostEstimate(flops=flops, bytes_accessed=2_000_000_000, transcendentals=0),
    )(*arrays, *after)


def adam_update(weight, gradient, first_old, second_old, rate_value, decay_rate):
    first_new = BETA_ONE * first_old + (1.0 - BETA_ONE) * gradient
    second_new = BETA_TWO * second_old + (1.0 - BETA_TWO) * gradient * gradient
    weight_full = weight.astype(jnp.float32)
    ratio = (
        first_new
        / (1.0 - BETA_ONE**STEP)
        / (jnp.sqrt(second_new / (1.0 - BETA_TWO**STEP)) + ADAM_EPS)
    )
    return (first_new, second_new, weight_full - rate_value * (ratio + decay_rate * weight_full))


def on_device(
    tokens,
    cotangent,
    routes,
    qkv_weight,
    out_weight,
    norm_gain,
    bias_rows,
    router_weight,
    expand_weight,
    shrink_weight,
    expert_bias,
    *moments,
):
    f32, bf = jnp.float32, jnp.bfloat16
    core = lax.axis_index(CORE)
    core_word = (core.astype(jnp.int32).reshape(1), "smem", None)
    micro, rows, width = tokens.shape

    def all_of(array):
        return (array, None, None)

    attn_own = jnp.concatenate(
        [qkv_weight, out_weight, norm_gain.T, bias_rows.T, router_weight, jnp.zeros((6, 118), bf)], 1
    )
    ebias_own = jnp.pad(expert_bias, [(0, 0), (0, 2)]).reshape(1, 96)
    attn_own = jnp.concatenate(
        [attn_own, jnp.pad(ebias_own, [(0, 1), (3072, 32)])], 0
    )
    mine = chips_gather(attn_own).reshape(64, 8, 3200)
    other = swap_cores(mine)

    w1_own = pad_rows(expand_weight, 8).reshape(3, 8, 4, 768).transpose(0, 2, 1, 3)
    expert_own = jnp.concatenate([shrink_weight.reshape(3, 3, 8, 768), w1_own], 1)
    expert_whole = lax.all_gather(expert_own[None], DEV, axis=0, tiled=True)

    def column(array, k, n=768):
        return (array, (64, 8, n), lambda *_: (0, 0, k))

    def columns(array):
        return (array, (64, 8, 768), lambda j: (0, 0, j))

    hot = (routes[:, :, :, None] == jnp.arange(3, dtype=jnp.int32)).astype(f32)
    member = jnp.sum(hot, 2).reshape(micro * rows, 3)
    lower = jnp.arange(micro * rows)[:, None] >= jnp.arange(micro * rows)[None, :]
    position = jnp.dot(lower.astype(bf), member.astype(bf), preferred_element_type=f32) - 1.0
    slots = jnp.where(member > 0, position, -1.0).astype(jnp.int32).reshape(micro, rows, 3)
    slot_rows = slots.transpose(0, 2, 1)

    spread = (
        (jnp.arange(width) // 6 * 8 + jnp.arange(width) % 6)[:, None] == jnp.arange(1024)[None, :]
    ).astype(bf)

    of_device = (jnp.arange(3840)[:, None] % 30 == jnp.arange(128)[None, :]).astype(bf)

    qkv, attn_wide, small, ebias = call(
        qkv_kernel,
        (3,),
        [
            core_word, columns(mine), columns(other), column(mine, 24, 128),
            column(other, 24, 128), all_of(spread), all_of(tokens), all_of(of_device),
        ],
        [
            ((micro, rows, 3 * width), bf, (micro, rows, 768), lambda j: (0, 0, j)),
            ((micro, rows, 1024), bf, None, None),
            ((128, width), f32, None, None),
            ((3, 1, 3840), f32, None, None),
        ],
        flops=2 * 394 * 1024 * 3000,
    )

    def one(array):
        return (array, (None, *array.shape[1:]), lambda b: (b, 0, 0))

    def one_out(n, kind):
        return ((micro, rows, n), kind, (None, rows, n), lambda b: (b, 0, 0))

    attended, middle, expert_input, prob, gates = call(
        attend_kernel,
        (micro,),
        [
            core_word, column(mine, 3), column(other, 3), one(qkv), one(tokens), one(routes),
            all_of(small), all_of(spread),
        ],
        [
            one_out(1024, bf), one_out(width, f32), one_out(1024, bf), one_out(3, f32),
            one_out(3, f32),
        ],
        [pltpu.VMEM((rows, width), bf)],
        flops=2 * 394 * 1024 * 2400,
    )

    output = middle
    wide_grad = None
    gate_grads, inner, outer, rings = [], [], [], []

    follow = ()
    for e in range(3):
        own, send, db1, db2, output, wide_grad, gg = call(
            functools.partial(expert_kernel, e),
            (4,),
            [
                core_word,
                (expert_whole, (32, None, 3, 8, 768), lambda i, e=e: (i, e, 0, 0, 0)),
                (expert_whole, (128, None, 1, 8, 768), lambda i, e=e: (0, e, 3 + i, 0, 0)),
                (ebias, (None, 1, 768), lambda i, e=e: (e, 0, i)),
                (ebias, (None, 1, 768), lambda i, e=e: (e, 0, 4)),
                all_of(expert_input), all_of(cotangent), all_of(slot_rows), all_of(slots),
                all_of(gates), all_of(output),
            ]
            + ([all_of(wide_grad)] if e else []),
            [
                ((64, 7, 8, 768), bf, "any", None),
                ((64, 7, 8, 768), bf, "any", None),
                ((1, 3072), f32, (1, 768), lambda i: (0, i)),
                ((1, 768), f32, None, None),
                ((micro, rows, width), f32, None, None),
                ((micro, rows, 1024), f32, None, None),
                ((micro, rows, 1), f32, None, None),
            ],
            [
                pltpu.VMEM((SLOTS, 1024), bf),
                pltpu.VMEM((1024, SLOTS), bf),
                pltpu.VMEM((SLOTS, 768), bf),
                pltpu.VMEM((SLOTS, 768), f32),
                pltpu.VMEM((SLOTS, 1024), f32),
                pltpu.VMEM((2, 64, 7, 8, 768), bf),
                pltpu.SemaphoreType.DMA((4, 4)),
            ],
            after=follow,
            flops=6 * 2 * SLOTS * 900 * 3072,
        )
        gate_grads.append(gg)
        inner.append(db1)
        outer.append(db2)
        if e == 1:
            *follow, send = next_round(rings, (gg,), (send,))
        elif e == 2:
            *follow, send = next_round(rings, (gg,), (send,))
        rings.append(Ring(own, swap_cores(send), e))

    middle_grad, attended_grad, own_out, send_out, small_grad = call(
        route_back_kernel,
        (1,),
        [
            core_word, column(mine, 3), column(other, 3), all_of(wide_grad),
            all_of(gate_grads[0]), all_of(gate_grads[1]), all_of(gate_grads[2]), all_of(prob),
            all_of(gates), all_of(slots), all_of(middle), all_of(cotangent), all_of(attended),
            all_of(small),
            all_of(spread),
        ],
        [
            ((micro, rows, width), f32, None, None),
            ((micro, rows, width), bf, None, None),
            ((64, 8, 768), bf, None, None),
            ((64, 8, 768), bf, None, None),
            ((8, width), f32, None, None),
        ],
        after=follow,
        flops=2 * 394 * 1024 * 4000,
    )
    qkv_grads = []
    follow = next_round(rings, (small_grad,))
    for b in range(micro):
        qkv_grads.append(
            call(
                attend_back_kernel,
                (1,),
                [
                    (qkv, (None, rows, 3 * width), lambda _, b=b: (b, 0, 0)),
                    (attended_grad, (None, rows, width), lambda _, b=b: (b, 0, 0)),
                ],
                [((rows, 3 * width), bf, None, None)],
                after=qkv_grads if b else follow,
                flops=2 * 197 * 1024 * 4000,
            )[0]
        )
    own_qkv, send_qkv, own_small, send_small, input_grad = call(
        qkv_back_kernel,
        (3,),
        [
            core_word, columns(mine), columns(other),
            *[(grad, (rows, 768), lambda j: (0, j)) for grad in qkv_grads],
            all_of(attn_wide), all_of(tokens), all_of(middle_grad), all_of(small),
            all_of(small_grad), *[all_of(a) for a in inner], *[all_of(a) for a in outer],
            all_of(of_device), all_of(spread),
        ],
        [
            ((64, 8, 3 * width), bf, (64, 8, 768), lambda j: (0, 0, j)),
            ((64, 8, 3 * width), bf, (64, 8, 768), lambda j: (0, 0, j)),
            ((64, 8, 128), bf, None, None),
            ((64, 8, 128), bf, None, None),
            ((micro, rows, width), f32, None, None),
        ],
        [pltpu.VMEM((micro, rows, 1024), f32), pltpu.VMEM((128, width), f32)],
        after=next_round(rings, qkv_grads[1:]),
        flops=2 * 394 * 1024 * 5000,
    )

    expert_sums = [rings[0].total()]
    next_round(rings[1:], (own_small, expert_sums[0]))
    expert_sums.append(rings[1].total())
    def chips_part(n):
        return (16, 8, n), lambda i: (i, 0, 0)

    parts = ((own_qkv, send_qkv), (own_out, send_out), (own_small, send_small))
    pair = call(
        pair_kernel,
        (4,),
        [
            (a, *chips_part(own.shape[2])) for own, send in parts for a in (own, swap_cores(send))
        ],
        [((64, 8, 3200), bf, *chips_part(3200))],
        after=expert_sums[1:2],
    )[0]
    next_round(rings[2:], (pair, expert_sums[1]))
    expert_sums.append(rings[2].total())
    attn_sum = call(
        sum_kernel,
        (1,),
        [all_of(lax.all_to_all(pair, CHIPS, 0, 0, tiled=True))],
        [((8, 3200), f32, None, None)],
    )[0]
    ebias_sum = attn_sum[6, 3072:3168].reshape(3, 32)[:, :30]
    attn_sum = attn_sum[:6]
    small_sum = attn_sum[:, 3072:]
    gain_sum, shift_sum, router_sum = small_sum[:, :2].T, small_sum[:, 2:7].T, small_sum[:, 7:10]
    expert_sums = jnp.stack(expert_sums)
    expand_sum = expert_sums[:, :4, :6].transpose(0, 2, 1, 3).reshape(3, 6, 3072)
    shrink_sum = expert_sums[:, 4:].reshape(3, 24, 768)

    weights_all = (
        qkv_weight,
        out_weight,
        norm_gain,
        bias_rows,
        router_weight,
        expand_weight,
        shrink_weight,
        expert_bias,
    )
    grads_all = (
        attn_sum[:, :2304],
        attn_sum[:, 2304:3072],
        gain_sum,
        shift_sum,
        router_sum,
        expand_sum,
        shrink_sum,
        ebias_sum,
    )
    results = [output, input_grad]
    for k in range(8):
        results.extend(
            adam_update(
                weights_all[k], grads_all[k], moments[k], moments[8 + k], RATES[k], DECAYS[k]
            )
        )
    return tuple(results)


def solution(mesh):
    split = Mesh(mesh.devices.reshape(4, 4, 4, 2), ("dev_0", "dev_1", "dev_2", "dev_3"))
    placed = (
        P(None, DEV, None),
        P(None, DEV, None),
        P(None, DEV, None),
        P(DEV, None),
        P(DEV, None),
        P(None, DEV),
        P(None, DEV),
        P(DEV, None),
        P(None, DEV, None),
        P(None, DEV, None),
        P(None, DEV),
        P(DEV, None),
        P(DEV, None),
        P(None, DEV),
        P(None, DEV),
        P(DEV, None),
        P(None, DEV, None),
        P(None, DEV, None),
        P(None, DEV),
        P(DEV, None),
        P(DEV, None),
        P(None, DEV),
        P(None, DEV),
        P(DEV, None),
        P(None, DEV, None),
        P(None, DEV, None),
        P(None, DEV),
    )
    return jax.shard_map(
        on_device,
        mesh=split,
        in_specs=placed,
        out_specs=(
            P(None, DEV, None),
            P(None, DEV, None),
            P(DEV, None),
            P(DEV, None),
            P(DEV, None),
            P(DEV, None),
            P(DEV, None),
            P(DEV, None),
            P(None, DEV),
            P(None, DEV),
            P(None, DEV),
            P(None, DEV),
            P(None, DEV),
            P(None, DEV),
            P(DEV, None),
            P(DEV, None),
            P(DEV, None),
            P(None, DEV, None),
            P(None, DEV, None),
            P(None, DEV, None),
            P(None, DEV, None),
            P(None, DEV, None),
            P(None, DEV, None),
            P(None, DEV),
            P(None, DEV),
            P(None, DEV),
        ),
        check_vma=False,
    )
```

```python
import functools

import jax
import jax.numpy as jnp
from jax import lax
from jax.experimental import pallas as pl
from jax.experimental.pallas import tpu as pltpu
from jax.sharding import Mesh
from jax.sharding import PartitionSpec as P

HEAD = 64
SEQ = 197
STEP = 10
CAP = 133
CHIPS = ("dev_0", "dev_1", "dev_2")
CORE = "dev_3"
DEV = ("dev_0", "dev_1", "dev_2", "dev_3")


NORM_EPS = 1e-06
ADAM_EPS = 1e-08
BETA_ONE = 0.9
BETA_TWO = 0.95
ROOT_HALF = 0.7071067811865476
INV_ROOT_TAU = 0.3989422804014327
RATES = (0.04, 0.2, 0.4, 0.04, 0.03, 0.04, 0.05, 0.04)
DECAYS = (0.1, 0.1, 0.0, 0.0, 0.1, 0.1, 0.1, 0.0)


def norm_parts(values):
    average = jnp.mean(values, -1, keepdims=True)
    centred = values - average
    inverse = lax.rsqrt(jnp.mean(centred * centred, -1, keepdims=True) + NORM_EPS)
    return (centred * inverse, inverse)


def norm_back(grad_norm, normed, inverse):
    return inverse * (
        grad_norm
        - jnp.mean(grad_norm, -1, keepdims=True)
        - normed * jnp.mean(grad_norm * normed, -1, keepdims=True)
    )


def softmax_rows(logits):
    shifted = jnp.exp(logits - jnp.max(logits, -1, keepdims=True))
    return shifted / jnp.sum(shifted, -1, keepdims=True)


def swap_cores(x):
    return lax.ppermute(x, CORE, [(0, 1), (1, 0)])


def pad_rows(x, length):
    return jnp.pad(x, [(0, 0)] * (x.ndim - 2) + [(0, length - x.shape[-2]), (0, 0)])


def ring_pairs():
    up = [(2 * i, 2 * ((i + 1) % 4)) for i in range(4)]
    return up + [(2 * i + 1, 2 * ((i - 1) % 4) + 1) for i in range(4)]


def chips_gather(x):
    sign = 1 - 2 * lax.axis_index(CORE)
    moving = lax.all_to_all(jnp.broadcast_to(x, (16, *x.shape)), CHIPS[1:], 0, 0, tiled=True)
    whole = jnp.zeros((4, *moving.shape), x.dtype)
    for step in range(4):
        index = lax.rem(lax.axis_index(CHIPS[0]) - sign * step + 4, 4)
        whole = lax.dynamic_update_index_in_dim(whole, moving, index, 0)
        if step < 3:
            moving = lax.ppermute(moving, (CHIPS[0], CORE), ring_pairs())
    return whole


def round_kernel(sizes, carried, index_ref, *refs):
    outs = refs[len(refs) - carried - len(sizes) : len(refs) - carried]
    at = 0
    for size, out_ref in zip(sizes, outs):
        total = sum([refs[at + k][...].astype(jnp.float32) for k in range(size)])
        out_ref[...] = total.astype(jnp.bfloat16)
        at += size


class Ring:
    def __init__(self, terms, *axes):
        self.shape = terms[0].shape[1:]
        self.terms = [a.reshape(4, 4, 4, *self.shape) for a in terms]
        self.names, self.axes = list(CHIPS), [CHIPS[k] for k in axes]
        self.step, self.piece = 0, None

    def place(self):
        return self.names.index(self.axes[0])

    def pass_on(self):
        return lax.ppermute(self.piece, (self.axes[0], CORE), ring_pairs())

    def advance(self, piece):
        self.step, self.piece = self.step + 1, piece
        if self.step == 4:
            self.names.remove(self.axes.pop(0))
            self.step, self.terms = 0, [piece]

    def total(self):
        return totals([self])[0]


def totals(rings):
    blocks = jnp.concatenate([r.piece.reshape(-1, *r.shape) for r in rings], 1)
    blocks = lax.all_to_all(blocks, tuple(rings[0].names), 0, 0, tiled=True)
    return jnp.split(jnp.sum(blocks.astype(jnp.float32), 0), len(rings))


def next_round(rings, after=(), carry=()):
    sign = 1 - 2 * lax.axis_index(CORE)
    index, arrays, specs, sizes = [], [], [], []
    outs = []
    for n, ring in enumerate(rings):
        index.append(lax.rem(lax.axis_index(ring.axes[0]) - sign * (1 + ring.step) + 8, 4))
        others = (1, 4)[: len(ring.names) - 1]
        block, place = list(others), ring.place()
        block.insert(place, None)
        tail = (0,) * (len(ring.shape) + len(others) - 1)

        def where(g, index_ref, place=place, n=n, tail=tail):
            at = [g, *tail]
            at.insert(place, index_ref[n])
            return tuple(at)

        moved = pl.BlockSpec((*others, *ring.shape), lambda g, _, tail=tail: (g, *tail))
        arrays += ring.terms
        specs += [pl.BlockSpec((*block, *ring.shape), where)] * len(ring.terms)
        sizes.append(len(ring.terms) + (1 if ring.step else 0))
        if ring.step:
            arrays.append(ring.pass_on())
            specs.append(moved)
        shape = (*(4,) * len(others), *ring.shape)
        outs.append((jax.ShapeDtypeStruct(shape, jnp.bfloat16), moved))
    at = 1 + len(arrays) + len(after)
    *pieces, = pl.pallas_call(
        functools.partial(round_kernel, sizes, len(carry)),
        grid_spec=pltpu.PrefetchScalarGridSpec(
            num_scalar_prefetch=1,
            grid=(4,),
            in_specs=specs + [pl.BlockSpec(memory_space=pl.ANY)] * (len(after) + len(carry)),
            out_specs=[spec for _, spec in outs]
            + [pl.BlockSpec(memory_space=pl.ANY)] * len(carry),
        ),
        out_shape=[shape for shape, _ in outs]
        + [jax.ShapeDtypeStruct(a.shape, a.dtype) for a in carry],
        input_output_aliases={at + k: len(outs) + k for k in range(len(carry))},
        compiler_params=pltpu.CompilerParams(vmem_limit_bytes=58 * 1024 * 1024),
        cost_estimate=pl.CostEstimate(
            flops=0, bytes_accessed=5_500_000 * len(rings), transcendentals=0
        ),
    )(jnp.stack(index).astype(jnp.int32), *arrays, *after, *carry)
    for ring, piece in zip(rings, pieces):
        ring.advance(piece)
    return tuple(pieces)


def gelu_both(z):
    half = 0.5 * (1.0 + lax.erf(z * ROOT_HALF))
    return z * half, half + z * jnp.exp(-0.5 * z * z) * INV_ROOT_TAU


SLOTS = 272


def mm(a, b, dims):
    return lax.dot_general(a, b, (dims, ((), ())), preferred_element_type=jnp.float32)


def two_terms(x):
    high = x.astype(jnp.bfloat16)
    return high, (x - high.astype(jnp.float32)).astype(jnp.bfloat16)


def to_wide(core, mine, other):
    mine, other = mine.astype(jnp.float32), other.astype(jnp.float32)
    both = jnp.stack([jnp.where(core == 0, mine, other), jnp.where(core == 0, other, mine)], 1)
    return both.reshape(1024, both.shape[-1]).astype(jnp.bfloat16)


def by_core(core, x, own_ref, send_ref):
    parts = x.reshape(own_ref.shape[0], 2, *own_ref.shape[1:])
    own_ref[...] = jnp.where(core == 0, parts[:, 0], parts[:, 1]).astype(jnp.bfloat16)
    send_ref[...] = jnp.where(core == 0, parts[:, 1], parts[:, 0]).astype(jnp.bfloat16)


def spread_out(x, spread):
    return mm(x, spread, ((1,), (0,))).astype(jnp.bfloat16)


def pull_in(x, spread):
    high, low = two_terms(x)
    return mm(high, spread, ((1,), (1,))) + mm(low, spread, ((1,), (1,)))


def ones_where(mask):
    return mask.astype(jnp.float32).astype(jnp.bfloat16)


def biases_of_devices():
    device = lax.broadcasted_iota(jnp.int32, (128, 3840), 0)
    value = lax.broadcasted_iota(jnp.int32, (128, 3840), 1)
    return (value >= 30 * device) & (value < 30 * device + 30)


def spare_rows():
    place = lax.broadcasted_iota(jnp.int32, (1024, 128), 0)
    return ones_where(place == 8 * lax.broadcasted_iota(jnp.int32, (1024, 128), 1) + 6)


def qkv_kernel(
    core_ref, mine_ref, other_ref, small_mine_ref, small_other_ref, spread_ref, tokens_ref,
    of_device_ref, qkv_ref, wide_ref, small_ref, ebias_ref,
):
    j = pl.program_id(0)
    core = core_ref[0]

    @pl.when(j == 0)
    def _():
        small = to_wide(core, small_mine_ref[...], small_other_ref[...])
        small_ref[...] = mm(small, spread_ref[...], ((0,), (1,)))
        blocks = mm(spare_rows(), small, ((0,), (0,))).astype(jnp.bfloat16)
        for e in range(3):
            spaced = mm(blocks[:, 32 * e : 32 * e + 32], of_device_ref[:, :32], ((1,), (1,)))
            ebias_ref[e] = jnp.sum(jnp.where(biases_of_devices(), spaced, 0.0), 0, keepdims=True)
        for b in range(2):
            normed, _ = norm_parts(tokens_ref[b].astype(jnp.float32))
            rows = (normed * small_ref[0:1] + small_ref[2:3]).astype(jnp.bfloat16)
            wide_ref[b] = spread_out(rows, spread_ref[...])

    weight = to_wide(core, mine_ref[...], other_ref[...])
    bias = jnp.where(j == 0, small_ref[4:5], jnp.where(j == 1, 0.0, small_ref[5:6]))
    for b in range(2):
        qkv_ref[b] = (mm(wide_ref[b], weight, ((1,), (0,))) + bias).astype(jnp.bfloat16)


def head_probs(query, key):
    scores = mm(query, key, ((1,), (1,))) * (HEAD ** (-0.5))
    return softmax_rows(scores)


def attend_kernel(
    core_ref, mine_ref, other_ref, qkv_ref, tokens_ref, routes_ref, small_ref, spread_ref,
    attended_ref, middle_ref, input_ref, prob_ref, gate_ref, kept,
):
    core = core_ref[0]
    width = tokens_ref.shape[-1]
    for pair in range(width // (2 * HEAD)):
        parts = []
        for h in (2 * pair, 2 * pair + 1):
            query, key, value = [
                qkv_ref[:, k * width + h * HEAD : k * width + (h + 1) * HEAD] for k in range(3)
            ]
            weights = head_probs(query, key).astype(jnp.bfloat16)
            parts.append(mm(weights, value, ((1,), (0,))))
        kept[:, pair * 128 : pair * 128 + 128] = jnp.concatenate(parts, 1).astype(jnp.bfloat16)
    spread = spread_ref[...]
    attended = spread_out(kept[...], spread)
    attended_ref[...] = attended
    weight = to_wide(core, mine_ref[...], other_ref[...])
    branch = mm(attended, weight, ((1,), (0,))) + small_ref[6:7]
    middle = tokens_ref[...].astype(jnp.float32) + branch
    middle_ref[...] = middle
    normed, _ = norm_parts(middle)
    rows = (normed * small_ref[1:2] + small_ref[3:4]).astype(jnp.bfloat16)
    input_ref[...] = spread_out(rows, spread)
    logits = mm(rows, small_ref[7:10].astype(jnp.bfloat16), ((1,), (1,)))
    prob = softmax_rows(logits)
    prob_ref[...] = prob
    experts = lax.broadcasted_iota(jnp.int32, prob.shape, 1)
    routes = routes_ref[...]
    member = ((experts == routes[:, 0:1]) | (experts == routes[:, 1:2])).astype(jnp.float32)
    chosen = member * prob
    gate_ref[...] = chosen / jnp.sum(chosen, 1, keepdims=True)


def expert_kernel(
    e, core_ref, w2_ref, w1_ref, b1_ref, b2_ref, x_ref, cot_ref, slot_row_ref, slot_col_ref,
    gate_ref, out_in_ref, *rest,
):
    (
        own_ref, send_ref, db1_ref, db2_ref, out_ref, dx_ref, gg_ref,
        xs, xts, rs, rows_acc, dx_acc, kept, sems,
    ) = rest[-14:]
    dx_in_ref = rest[0] if e > 0 else None
    i = pl.program_id(0)
    core = core_ref[0]
    tokens = x_ref.shape[1]

    @pl.when(i == 0)
    def _():
        taken, grads = 0.0, 0.0
        for b in range(2):
            slots = lax.broadcasted_iota(jnp.int32, (SLOTS, tokens), 0)
            pick = ones_where(slots == slot_row_ref[b, e : e + 1, :])
            taken += mm(pick, x_ref[b], ((1,), (0,)))
            scaled = (gate_ref[b][:, e : e + 1] * cot_ref[b]).astype(jnp.bfloat16)
            grads += mm(pick, scaled, ((1,), (0,)))
        xs[...] = taken.astype(jnp.bfloat16)
        xts[...] = taken.T.astype(jnp.bfloat16)
        rs[...] = grads.astype(jnp.bfloat16)
        db2_ref[...] = jnp.sum(grads, 0, keepdims=True)
        rows_acc[...] = jnp.zeros_like(rows_acc) + b2_ref[...]
        dx_acc[...] = jnp.zeros_like(dx_acc)

    x = xs[...]
    r = rs[...]
    w1 = w1_ref[...].astype(jnp.float32).reshape(1024, 768).astype(jnp.bfloat16)
    w2 = w2_ref[...].astype(jnp.float32).reshape(768, 768).astype(jnp.bfloat16)
    hidden = mm(x, w1, ((1,), (0,))) + b1_ref[...]
    act, slope = gelu_both(hidden)
    act = act.astype(jnp.bfloat16)
    rows_acc[...] += mm(act, w2, ((1,), (0,)))
    dw2 = mm(act, r, ((0,), (0,))).reshape(16, 2, 3, 8, 768)
    for c in range(2):
        kept[c, pl.ds(pl.multiple_of(16 * i, 16), 16), 4:7] = dw2[:, c].astype(jnp.bfloat16)
    dh = mm(r, w2, ((1,), (1,))) * slope
    dh = dh.astype(jnp.bfloat16)
    db1_ref[...] = jnp.sum(dh.astype(jnp.float32), 0, keepdims=True)
    dw1 = mm(xts[...], dh, ((1,), (0,))).reshape(64, 2, 1, 8, 768)
    for c in range(2):
        kept[c, :, pl.ds(i, 1)] = dw1[:, c].astype(jnp.bfloat16)
    dx_acc[...] += mm(dh, w1, ((1,), (1,)))

    def copies(step):
        parts = [
            (slice(None), pl.ds(step, 1)),
            (pl.ds(pl.multiple_of(16 * step, 16), 16), pl.ds(4, 3)),
        ]
        pairs = [(kept.at[core], own_ref), (kept.at[1 - core], send_ref)]
        return [
            pltpu.make_async_copy(source.at[part], ref.at[part], sems.at[step, 2 * k + m])
            for k, (source, ref) in enumerate(pairs)
            for m, part in enumerate(parts)
        ]

    for copy in copies(i):
        copy.start()

    @pl.when(i == pl.num_programs(0) - 1)
    def _():
        rows_terms = two_terms(rows_acc[...])
        dx_terms = two_terms(dx_acc[...])
        for b in range(2):
            slots = lax.broadcasted_iota(jnp.int32, (tokens, SLOTS), 1)
            put = ones_where(slots == slot_col_ref[b][:, e : e + 1])
            rows = sum([mm(put, term, ((1,), (0,))) for term in rows_terms])
            out_ref[b] = out_in_ref[b] + gate_ref[b][:, e : e + 1] * rows
            gg_ref[b] = jnp.sum(rows * cot_ref[b], 1, keepdims=True)
            grad = sum([mm(put, term, ((1,), (0,))) for term in dx_terms])
            dx_ref[b] = grad if e == 0 else dx_in_ref[b] + grad
        for step in range(4):
            for copy in copies(step):
                copy.wait()


def route_back_kernel(
    core_ref, mine_ref, other_ref, dx_ref, gg0_ref, gg1_ref, gg2_ref, prob_ref, gate_ref,
    slots_ref, middle_ref, cot_ref, attended_ref, small_ref, spread_ref, *rest,
):
    grad_ref, attended_grad_ref, own_ref, send_ref, small_out_ref = rest[-5:]
    core = core_ref[0]
    spread = spread_ref[...]
    weight = to_wide(core, mine_ref[...], other_ref[...])
    router = small_ref[7:10].astype(jnp.bfloat16)
    total, sums, router_grad = 0.0, [0.0, 0.0, 0.0], 0.0
    for b in range(2):
        prob, gate = prob_ref[b], gate_ref[b]
        experts = lax.broadcasted_iota(jnp.int32, prob.shape, 1)
        gate_grad = jnp.where(
            experts == 0, gg0_ref[b], jnp.where(experts == 1, gg1_ref[b], gg2_ref[b])
        )
        member = (slots_ref[b] >= 0).astype(jnp.float32)
        chosen = jnp.sum(member * prob, 1, keepdims=True)
        share = jnp.sum(gate_grad * gate, 1, keepdims=True)
        prob_grad = member * (gate_grad - share) / chosen
        logit_grad = prob * (prob_grad - jnp.sum(prob * prob_grad, 1, keepdims=True))
        logit_grad = logit_grad.astype(jnp.bfloat16)
        normed, inverse = norm_parts(middle_ref[b])
        rows = (normed * small_ref[1:2] + small_ref[3:4]).astype(jnp.bfloat16)
        router_grad += mm(logit_grad, rows, ((0,), (0,)))
        grad = pull_in(dx_ref[b], spread) + mm(logit_grad, router, ((1,), (0,)))
        sums[0] += jnp.sum(grad * normed, 0, keepdims=True)
        sums[1] += jnp.sum(grad, 0, keepdims=True)
        grad = cot_ref[b] + norm_back(grad * small_ref[1:2], normed, inverse)
        grad_ref[b] = grad
        branch = grad.astype(jnp.bfloat16)
        sums[2] += jnp.sum(branch.astype(jnp.float32), 0, keepdims=True)
        total += mm(attended_ref[b], branch, ((0,), (0,)))
        wide = mm(branch, weight, ((1,), (1,))).astype(jnp.bfloat16)
        attended_grad_ref[b] = mm(wide, spread, ((1,), (1,))).astype(jnp.bfloat16)
    by_core(core, total, own_ref, send_ref)
    for k in range(3):
        small_out_ref[k : k + 1] = sums[k]
    small_out_ref[3:6] = router_grad


def attend_back_kernel(qkv_ref, grad_ref, *rest):
    out_ref = rest[-1]
    width = grad_ref.shape[-1]
    scaling = HEAD ** (-0.5)
    for pair in range(width // (2 * HEAD)):
        parts = [[], [], []]
        for h in (2 * pair, 2 * pair + 1):
            query, key, value = [
                qkv_ref[:, k * width + h * HEAD : k * width + (h + 1) * HEAD] for k in range(3)
            ]
            grad = grad_ref[:, h * HEAD : (h + 1) * HEAD]
            probs = head_probs(query, key)
            prob_grad = mm(grad, value, ((1,), (1,)))
            score_grad = probs * (prob_grad - jnp.sum(probs * prob_grad, 1, keepdims=True))
            score_grad = score_grad.astype(jnp.bfloat16)
            parts[0].append(mm(score_grad, key, ((1,), (0,))) * scaling)
            parts[1].append(mm(score_grad, query, ((0,), (0,))) * scaling)
            parts[2].append(mm(probs.astype(jnp.bfloat16), grad, ((0,), (0,))))
        for k in range(3):
            at = k * width + pair * 128
            out_ref[:, at : at + 128] = jnp.concatenate(parts[k], 1).astype(jnp.bfloat16)


def qkv_back_kernel(
    core_ref, mine_ref, other_ref, qkv_grad0_ref, qkv_grad1_ref, wide_ref, tokens_ref, grad_ref,
    small_ref, early_ref, in0_ref, in1_ref, in2_ref, out0_ref, out1_ref, out2_ref, of_device_ref,
    spread_ref, *rest,
):
    own_ref, send_ref, small_own_ref, small_send_ref, input_grad_ref, acc, sums = rest[-7:]
    j = pl.program_id(0)
    core = core_ref[0]
    weight = to_wide(core, mine_ref[...], other_ref[...])

    @pl.when(j == 0)
    def _():
        acc[...] = jnp.zeros_like(acc)
        sums[...] = jnp.zeros_like(sums)
        sums[1:2] = early_ref[0:1]
        sums[3:4] = early_ref[1:2]
        sums[6:10] = early_ref[2:6]

    total, bias = 0.0, 0.0
    for b in range(2):
        grad = (qkv_grad0_ref, qkv_grad1_ref)[b][...]
        total += mm(wide_ref[b], grad, ((0,), (0,)))
        bias += jnp.sum(grad.astype(jnp.float32), 0, keepdims=True)
        acc[b] += mm(grad, weight, ((1,), (1,)))
    by_core(core, total, own_ref, send_ref)

    @pl.when(j == 0)
    def _():
        sums[4:5] += bias

    @pl.when(j == 2)
    def _():
        sums[5:6] += bias
        spread = spread_ref[...]
        for b in range(2):
            normed, inverse = norm_parts(tokens_ref[b].astype(jnp.float32))
            grad = pull_in(acc[b], spread)
            sums[0:1] += jnp.sum(grad * normed, 0, keepdims=True)
            sums[2:3] += jnp.sum(grad, 0, keepdims=True)
            input_grad_ref[b] = grad_ref[b] + norm_back(grad * small_ref[0:1], normed, inverse)
        small = mm(spread, sums[...].astype(jnp.bfloat16), ((0,), (1,)))
        blocks = []
        for inner, outer in ((in0_ref, out0_ref), (in1_ref, out1_ref), (in2_ref, out2_ref)):
            biases = jnp.concatenate([inner[...], outer[...]], 1)
            spaced = jnp.where(biases_of_devices(), biases, 0.0).astype(jnp.bfloat16)
            blocks.append(mm(spaced, of_device_ref[...], ((1,), (0,)))[:, :32])
        blocks.append(jnp.zeros((128, 32), jnp.float32))
        blocks = jnp.concatenate(blocks, 1).astype(jnp.bfloat16)
        small += mm(spare_rows(), blocks, ((1,), (0,)))
        by_core(core, small, small_own_ref, small_send_ref)


def pair_kernel(own_qkv, got_qkv, own_out, got_out, own_small, got_small, *rest):
    out_ref = rest[-1]
    at = 0
    for own, got in ((own_qkv, got_qkv), (own_out, got_out), (own_small, got_small)):
        total = own[...].astype(jnp.float32) + got[...].astype(jnp.float32)
        out_ref[:, :, at : at + own.shape[2]] = total.astype(jnp.bfloat16)
        at += own.shape[2]


def call(kernel, grid, ins, outs, scratch=(), after=(), flops=0):
    def spec(shape, block, index):
        if block == "any":
            return pl.BlockSpec(memory_space=pl.ANY)
        if block is None:
            return pl.BlockSpec(shape, lambda *_: (0,) * len(shape))
        return pl.BlockSpec(block, index)

    in_specs = [
        pl.BlockSpec(memory_space=pltpu.SMEM)
        if block == "smem"
        else spec(array.shape, block, index)
        for array, block, index in ins
    ]
    in_specs += [pl.BlockSpec(memory_space=pl.ANY)] * len(after)
    arrays = [array for array, _, _ in ins]
    return pl.pallas_call(
        kernel,
        grid=grid,
        in_specs=in_specs,
        out_specs=[spec(shape, block, index) for shape, _, block, index in outs],
        out_shape=[jax.ShapeDtypeStruct(shape, kind) for shape, kind, _, _ in outs],
        scratch_shapes=list(scratch),
        compiler_params=pltpu.CompilerParams(vmem_limit_bytes=58 * 1024 * 1024),
        cost_estimate=pl.CostEstimate(flops=flops, bytes_accessed=2_000_000_000, transcendentals=0),
    )(*arrays, *after)


def adam_update(weight, gradient, first_old, second_old, rate_value, decay_rate):
    first_new = BETA_ONE * first_old + (1.0 - BETA_ONE) * gradient
    second_new = BETA_TWO * second_old + (1.0 - BETA_TWO) * gradient * gradient
    weight_full = weight.astype(jnp.float32)
    ratio = (
        first_new
        / (1.0 - BETA_ONE**STEP)
        / (jnp.sqrt(second_new / (1.0 - BETA_TWO**STEP)) + ADAM_EPS)
    )
    return (first_new, second_new, weight_full - rate_value * (ratio + decay_rate * weight_full))


def on_device(
    tokens,
    cotangent,
    routes,
    qkv_weight,
    out_weight,
    norm_gain,
    bias_rows,
    router_weight,
    expand_weight,
    shrink_weight,
    expert_bias,
    *moments,
):
    f32, bf = jnp.float32, jnp.bfloat16
    core = lax.axis_index(CORE)
    core_word = (core.astype(jnp.int32).reshape(1), "smem", None)
    micro, rows, width = tokens.shape

    def all_of(array):
        return (array, None, None)

    attn_own = jnp.concatenate(
        [qkv_weight, out_weight, norm_gain.T, bias_rows.T, router_weight, jnp.zeros((6, 118), bf)], 1
    )
    ebias_own = jnp.pad(expert_bias, [(0, 0), (0, 2)]).reshape(1, 96)
    attn_own = jnp.concatenate(
        [attn_own, jnp.pad(ebias_own, [(0, 1), (3072, 32)])], 0
    )
    mine = chips_gather(attn_own).reshape(64, 8, 3200)
    other = swap_cores(mine)

    w1_own = pad_rows(expand_weight, 8).reshape(3, 8, 4, 768).transpose(0, 2, 1, 3)
    expert_own = jnp.concatenate([shrink_weight.reshape(3, 3, 8, 768), w1_own], 1)
    expert_whole = lax.all_gather(expert_own[None], DEV, axis=0, tiled=True)

    def column(array, k, n=768):
        return (array, (64, 8, n), lambda *_: (0, 0, k))

    def columns(array):
        return (array, (64, 8, 768), lambda j: (0, 0, j))

    hot = (routes[:, :, :, None] == jnp.arange(3, dtype=jnp.int32)).astype(f32)
    member = jnp.sum(hot, 2).reshape(micro * rows, 3)
    lower = jnp.arange(micro * rows)[:, None] >= jnp.arange(micro * rows)[None, :]
    position = jnp.dot(lower.astype(bf), member.astype(bf), preferred_element_type=f32) - 1.0
    slots = jnp.where(member > 0, position, -1.0).astype(jnp.int32).reshape(micro, rows, 3)
    slot_rows = slots.transpose(0, 2, 1)

    spread = (
        (jnp.arange(width) // 6 * 8 + jnp.arange(width) % 6)[:, None] == jnp.arange(1024)[None, :]
    ).astype(bf)

    of_device = (jnp.arange(3840)[:, None] % 30 == jnp.arange(128)[None, :]).astype(bf)

    qkv, attn_wide, small, ebias = call(
        qkv_kernel,
        (3,),
        [
            core_word, columns(mine), columns(other), column(mine, 24, 128),
            column(other, 24, 128), all_of(spread), all_of(tokens), all_of(of_device),
        ],
        [
            ((micro, rows, 3 * width), bf, (micro, rows, 768), lambda j: (0, 0, j)),
            ((micro, rows, 1024), bf, None, None),
            ((128, width), f32, None, None),
            ((3, 1, 3840), f32, None, None),
        ],
        flops=2 * 394 * 1024 * 3000,
    )

    def one(array):
        return (array, (None, *array.shape[1:]), lambda b: (b, 0, 0))

    def one_out(n, kind):
        return ((micro, rows, n), kind, (None, rows, n), lambda b: (b, 0, 0))

    attended, middle, expert_input, prob, gates = call(
        attend_kernel,
        (micro,),
        [
            core_word, column(mine, 3), column(other, 3), one(qkv), one(tokens), one(routes),
            all_of(small), all_of(spread),
        ],
        [
            one_out(1024, bf), one_out(width, f32), one_out(1024, bf), one_out(3, f32),
            one_out(3, f32),
        ],
        [pltpu.VMEM((rows, width), bf)],
        flops=2 * 394 * 1024 * 2400,
    )

    output = middle
    wide_grad = None
    gate_grads, inner, outer, rings = [], [], [], []

    follow = ()
    for e in range(3):
        own, send, db1, db2, output, wide_grad, gg = call(
            functools.partial(expert_kernel, e),
            (4,),
            [
                core_word,
                (expert_whole, (32, None, 3, 8, 768), lambda i, e=e: (i, e, 0, 0, 0)),
                (expert_whole, (128, None, 1, 8, 768), lambda i, e=e: (0, e, 3 + i, 0, 0)),
                (ebias, (None, 1, 768), lambda i, e=e: (e, 0, i)),
                (ebias, (None, 1, 768), lambda i, e=e: (e, 0, 4)),
                all_of(expert_input), all_of(cotangent), all_of(slot_rows), all_of(slots),
                all_of(gates), all_of(output),
            ]
            + ([all_of(wide_grad)] if e else []),
            [
                ((64, 7, 8, 768), bf, "any", None),
                ((64, 7, 8, 768), bf, "any", None),
                ((1, 3072), f32, (1, 768), lambda i: (0, i)),
                ((1, 768), f32, None, None),
                ((micro, rows, width), f32, None, None),
                ((micro, rows, 1024), f32, None, None),
                ((micro, rows, 1), f32, None, None),
            ],
            [
                pltpu.VMEM((SLOTS, 1024), bf),
                pltpu.VMEM((1024, SLOTS), bf),
                pltpu.VMEM((SLOTS, 768), bf),
                pltpu.VMEM((SLOTS, 768), f32),
                pltpu.VMEM((SLOTS, 1024), f32),
                pltpu.VMEM((2, 64, 7, 8, 768), bf),
                pltpu.SemaphoreType.DMA((4, 4)),
            ],
            after=follow,
            flops=6 * 2 * SLOTS * 900 * 3072,
        )
        gate_grads.append(gg)
        inner.append(db1)
        outer.append(db2)
        if e == 1:
            *follow, send = next_round(rings, (gg,), (send,))
        elif e == 2:
            *follow, send = next_round(rings, (gg,), (send,))
        rings.append(Ring((own, swap_cores(send)), *((0, 1), (1, 2), (2, 1))[e]))

    middle_grad, attended_grad, own_out, send_out, small_grad = call(
        route_back_kernel,
        (1,),
        [
            core_word, column(mine, 3), column(other, 3), all_of(wide_grad),
            all_of(gate_grads[0]), all_of(gate_grads[1]), all_of(gate_grads[2]), all_of(prob),
            all_of(gates), all_of(slots), all_of(middle), all_of(cotangent), all_of(attended),
            all_of(small),
            all_of(spread),
        ],
        [
            ((micro, rows, width), f32, None, None),
            ((micro, rows, width), bf, None, None),
            ((64, 8, 768), bf, None, None),
            ((64, 8, 768), bf, None, None),
            ((8, width), f32, None, None),
        ],
        after=follow,
        flops=2 * 394 * 1024 * 4000,
    )
    qkv_grads = []
    follow = next_round(rings, (small_grad,))
    for b in range(micro):
        qkv_grads.append(
            call(
                attend_back_kernel,
                (1,),
                [
                    (qkv, (None, rows, 3 * width), lambda _, b=b: (b, 0, 0)),
                    (attended_grad, (None, rows, width), lambda _, b=b: (b, 0, 0)),
                ],
                [((rows, 3 * width), bf, None, None)],
                after=qkv_grads if b else follow,
                flops=2 * 197 * 1024 * 4000,
            )[0]
        )
    next_round(rings, qkv_grads[1:])
    follow = next_round(rings[:1])
    own_qkv, send_qkv, own_small, send_small, input_grad = call(
        qkv_back_kernel,
        (3,),
        [
            core_word, columns(mine), columns(other),
            *[(grad, (rows, 768), lambda j: (0, j)) for grad in qkv_grads],
            all_of(attn_wide), all_of(tokens), all_of(middle_grad), all_of(small),
            all_of(small_grad), *[all_of(a) for a in inner], *[all_of(a) for a in outer],
            all_of(of_device), all_of(spread),
        ],
        [
            ((64, 8, 3 * width), bf, (64, 8, 768), lambda j: (0, 0, j)),
            ((64, 8, 3 * width), bf, (64, 8, 768), lambda j: (0, 0, j)),
            ((64, 8, 128), bf, None, None),
            ((64, 8, 128), bf, None, None),
            ((micro, rows, width), f32, None, None),
        ],
        [pltpu.VMEM((micro, rows, 1024), f32), pltpu.VMEM((128, width), f32)],
        after=follow,
        flops=2 * 394 * 1024 * 5000,
    )

    follow = next_round(rings[1:], (own_small,))
    def chips_part(n):
        return (16, 8, n), lambda i: (i, 0, 0)

    parts = ((own_qkv, send_qkv), (own_out, send_out), (own_small, send_small))
    pair = call(
        pair_kernel,
        (4,),
        [
            (a, *chips_part(own.shape[2])) for own, send in parts for a in (own, swap_cores(send))
        ],
        [((64, 8, 3200), bf, *chips_part(3200))],
        after=follow,
    )[0]
    attn_ring = Ring((pair,), 0)
    for _ in range(3):
        next_round(rings, next_round([attn_ring]))
    next_round([attn_ring])
    attn_sum = attn_ring.total()
    next_round(rings[1:], (attn_ring.piece,))
    next_round(rings[2:], (attn_sum,))
    expert_sums = [rings[0].total(), *totals(rings[1:])]
    ebias_sum = attn_sum[6, 3072:3168].reshape(3, 32)[:, :30]
    attn_sum = attn_sum[:6]
    small_sum = attn_sum[:, 3072:]
    gain_sum, shift_sum, router_sum = small_sum[:, :2].T, small_sum[:, 2:7].T, small_sum[:, 7:10]
    expert_sums = jnp.stack(expert_sums)
    expand_sum = expert_sums[:, :4, :6].transpose(0, 2, 1, 3).reshape(3, 6, 3072)
    shrink_sum = expert_sums[:, 4:].reshape(3, 24, 768)

    weights_all = (
        qkv_weight,
        out_weight,
        norm_gain,
        bias_rows,
        router_weight,
        expand_weight,
        shrink_weight,
        expert_bias,
    )
    grads_all = (
        attn_sum[:, :2304],
        attn_sum[:, 2304:3072],
        gain_sum,
        shift_sum,
        router_sum,
        expand_sum,
        shrink_sum,
        ebias_sum,
    )
    results = [output, input_grad]
    for k in range(8):
        results.extend(
            adam_update(
                weights_all[k], grads_all[k], moments[k], moments[8 + k], RATES[k], DECAYS[k]
            )
        )
    return tuple(results)


def solution(mesh):
    split = Mesh(mesh.devices.reshape(4, 4, 4, 2), ("dev_0", "dev_1", "dev_2", "dev_3"))
    placed = (
        P(None, DEV, None),
        P(None, DEV, None),
        P(None, DEV, None),
        P(DEV, None),
        P(DEV, None),
        P(None, DEV),
        P(None, DEV),
        P(DEV, None),
        P(None, DEV, None),
        P(None, DEV, None),
        P(None, DEV),
        P(DEV, None),
        P(DEV, None),
        P(None, DEV),
        P(None, DEV),
        P(DEV, None),
        P(None, DEV, None),
        P(None, DEV, None),
        P(None, DEV),
        P(DEV, None),
        P(DEV, None),
        P(None, DEV),
        P(None, DEV),
        P(DEV, None),
        P(None, DEV, None),
        P(None, DEV, None),
        P(None, DEV),
    )
    return jax.shard_map(
        on_device,
        mesh=split,
        in_specs=placed,
        out_specs=(
            P(None, DEV, None),
            P(None, DEV, None),
            P(DEV, None),
            P(DEV, None),
            P(DEV, None),
            P(DEV, None),
            P(DEV, None),
            P(DEV, None),
            P(None, DEV),
            P(None, DEV),
            P(None, DEV),
            P(None, DEV),
            P(None, DEV),
            P(None, DEV),
            P(DEV, None),
            P(DEV, None),
            P(DEV, None),
            P(None, DEV, None),
            P(None, DEV, None),
            P(None, DEV, None),
            P(None, DEV, None),
            P(None, DEV, None),
            P(None, DEV, None),
            P(None, DEV),
            P(None, DEV),
            P(None, DEV),
        ),
        check_vma=False,
    )
```

```python
import functools

import jax
import jax.numpy as jnp
from jax import lax
from jax.experimental import pallas as pl
from jax.experimental.pallas import tpu as pltpu
from jax.sharding import Mesh
from jax.sharding import PartitionSpec as P

HEAD = 64
SEQ = 197
STEP = 10
CAP = 133
CHIPS = ("dev_0", "dev_1", "dev_2")
CORE = "dev_3"
DEV = ("dev_0", "dev_1", "dev_2", "dev_3")


NORM_EPS = 1e-06
ADAM_EPS = 1e-08
BETA_ONE = 0.9
BETA_TWO = 0.95
ROOT_HALF = 0.7071067811865476
INV_ROOT_TAU = 0.3989422804014327
RATES = (0.04, 0.2, 0.4, 0.04, 0.03, 0.04, 0.05, 0.04)
DECAYS = (0.1, 0.1, 0.0, 0.0, 0.1, 0.1, 0.1, 0.0)


def norm_parts(values):
    average = jnp.mean(values, -1, keepdims=True)
    centred = values - average
    inverse = lax.rsqrt(jnp.mean(centred * centred, -1, keepdims=True) + NORM_EPS)
    return (centred * inverse, inverse)


def norm_back(grad_norm, normed, inverse):
    return inverse * (
        grad_norm
        - jnp.mean(grad_norm, -1, keepdims=True)
        - normed * jnp.mean(grad_norm * normed, -1, keepdims=True)
    )


def softmax_rows(logits):
    shifted = jnp.exp(logits - jnp.max(logits, -1, keepdims=True))
    return shifted / jnp.sum(shifted, -1, keepdims=True)


def swap_cores(x):
    return lax.ppermute(x, CORE, [(0, 1), (1, 0)])


def pad_rows(x, length):
    return jnp.pad(x, [(0, 0)] * (x.ndim - 2) + [(0, length - x.shape[-2]), (0, 0)])


def ring_pairs():
    up = [(2 * i, 2 * ((i + 1) % 4)) for i in range(4)]
    return up + [(2 * i + 1, 2 * ((i - 1) % 4) + 1) for i in range(4)]


def chips_gather(x):
    sign = 1 - 2 * lax.axis_index(CORE)
    moving = lax.all_to_all(jnp.broadcast_to(x, (16, *x.shape)), CHIPS[1:], 0, 0, tiled=True)
    whole = jnp.zeros((4, *moving.shape), x.dtype)
    for step in range(4):
        index = lax.rem(lax.axis_index(CHIPS[0]) - sign * step + 4, 4)
        whole = lax.dynamic_update_index_in_dim(whole, moving, index, 0)
        if step < 3:
            moving = lax.ppermute(moving, (CHIPS[0], CORE), ring_pairs())
    return whole


def round_kernel(sizes, carried, index_ref, *refs):
    outs = refs[len(refs) - carried - len(sizes) : len(refs) - carried]
    at = 0
    for size, out_ref in zip(sizes, outs):
        total = sum([refs[at + k][...].astype(jnp.float32) for k in range(size)])
        out_ref[...] = total.astype(jnp.bfloat16)
        at += size


class Ring:
    def __init__(self, terms, *axes):
        self.shape = terms[0].shape[1:]
        self.terms = [a.reshape(4, 4, 4, *self.shape) for a in terms]
        self.names, self.axes = list(CHIPS), [CHIPS[k] for k in axes]
        self.step, self.piece = 0, None

    def place(self):
        return self.names.index(self.axes[0])

    def pass_on(self):
        return lax.ppermute(self.piece, (self.axes[0], CORE), ring_pairs())

    def advance(self, piece):
        self.step, self.piece = self.step + 1, piece
        if self.step == 4:
            self.names.remove(self.axes.pop(0))
            self.step, self.terms = 0, [piece]

    def total(self):
        return totals([self])[0]


def totals(rings):
    blocks = jnp.concatenate([r.piece.reshape(-1, *r.shape) for r in rings], 1)
    blocks = lax.all_to_all(blocks, tuple(rings[0].names), 0, 0, tiled=True)
    return jnp.split(jnp.sum(blocks.astype(jnp.float32), 0), len(rings))


def next_round(rings, after=(), carry=()):
    sign = 1 - 2 * lax.axis_index(CORE)
    index, arrays, specs, sizes = [], [], [], []
    outs = []
    for n, ring in enumerate(rings):
        index.append(lax.rem(lax.axis_index(ring.axes[0]) - sign * (1 + ring.step) + 8, 4))
        others = (1, 4)[: len(ring.names) - 1]
        block, place = list(others), ring.place()
        block.insert(place, None)
        tail = (0,) * (len(ring.shape) + len(others) - 1)

        def where(g, index_ref, place=place, n=n, tail=tail):
            at = [g, *tail]
            at.insert(place, index_ref[n])
            return tuple(at)

        moved = pl.BlockSpec((*others, *ring.shape), lambda g, _, tail=tail: (g, *tail))
        arrays += ring.terms
        specs += [pl.BlockSpec((*block, *ring.shape), where)] * len(ring.terms)
        sizes.append(len(ring.terms) + (1 if ring.step else 0))
        if ring.step:
            arrays.append(ring.pass_on())
            specs.append(moved)
        shape = (*(4,) * len(others), *ring.shape)
        outs.append((jax.ShapeDtypeStruct(shape, jnp.bfloat16), moved))
    at = 1 + len(arrays) + len(after)
    *pieces, = pl.pallas_call(
        functools.partial(round_kernel, sizes, len(carry)),
        grid_spec=pltpu.PrefetchScalarGridSpec(
            num_scalar_prefetch=1,
            grid=(4,),
            in_specs=specs + [pl.BlockSpec(memory_space=pl.ANY)] * (len(after) + len(carry)),
            out_specs=[spec for _, spec in outs]
            + [pl.BlockSpec(memory_space=pl.ANY)] * len(carry),
        ),
        out_shape=[shape for shape, _ in outs]
        + [jax.ShapeDtypeStruct(a.shape, a.dtype) for a in carry],
        input_output_aliases={at + k: len(outs) + k for k in range(len(carry))},
        compiler_params=pltpu.CompilerParams(vmem_limit_bytes=58 * 1024 * 1024),
        cost_estimate=pl.CostEstimate(
            flops=0, bytes_accessed=5_500_000 * len(rings), transcendentals=0
        ),
    )(jnp.stack(index).astype(jnp.int32), *arrays, *after, *carry)
    for ring, piece in zip(rings, pieces):
        ring.advance(piece)
    return tuple(pieces)


def gelu_both(z):
    half = 0.5 * (1.0 + lax.erf(z * ROOT_HALF))
    return z * half, half + z * jnp.exp(-0.5 * z * z) * INV_ROOT_TAU


SLOTS = 272


def mm(a, b, dims):
    return lax.dot_general(a, b, (dims, ((), ())), preferred_element_type=jnp.float32)


def two_terms(x):
    high = x.astype(jnp.bfloat16)
    return high, (x - high.astype(jnp.float32)).astype(jnp.bfloat16)


def to_wide(core, mine, other):
    mine, other = mine.astype(jnp.float32), other.astype(jnp.float32)
    both = jnp.stack([jnp.where(core == 0, mine, other), jnp.where(core == 0, other, mine)], 1)
    return both.reshape(1024, both.shape[-1]).astype(jnp.bfloat16)


def by_core(core, x, own_ref, send_ref):
    parts = x.reshape(own_ref.shape[0], 2, *own_ref.shape[1:])
    own_ref[...] = jnp.where(core == 0, parts[:, 0], parts[:, 1]).astype(jnp.bfloat16)
    send_ref[...] = jnp.where(core == 0, parts[:, 1], parts[:, 0]).astype(jnp.bfloat16)


def spread_out(x, spread):
    return mm(x, spread, ((1,), (0,))).astype(jnp.bfloat16)


def pull_in(x, spread):
    high, low = two_terms(x)
    return mm(high, spread, ((1,), (1,))) + mm(low, spread, ((1,), (1,)))


def ones_where(mask):
    return mask.astype(jnp.float32).astype(jnp.bfloat16)


def biases_of_devices():
    device = lax.broadcasted_iota(jnp.int32, (128, 3840), 0)
    value = lax.broadcasted_iota(jnp.int32, (128, 3840), 1)
    return (value >= 30 * device) & (value < 30 * device + 30)


def spare_rows():
    place = lax.broadcasted_iota(jnp.int32, (1024, 128), 0)
    return ones_where(place == 8 * lax.broadcasted_iota(jnp.int32, (1024, 128), 1) + 6)


def qkv_kernel(
    core_ref, mine_ref, other_ref, small_mine_ref, small_other_ref, spread_ref, tokens_ref,
    of_device_ref, qkv_ref, wide_ref, small_ref, ebias_ref,
):
    j = pl.program_id(0)
    core = core_ref[0]

    @pl.when(j == 0)
    def _():
        small = to_wide(core, small_mine_ref[...], small_other_ref[...])
        small_ref[...] = mm(small, spread_ref[...], ((0,), (1,)))
        blocks = mm(spare_rows(), small, ((0,), (0,))).astype(jnp.bfloat16)
        for e in range(3):
            spaced = mm(blocks[:, 32 * e : 32 * e + 32], of_device_ref[:, :32], ((1,), (1,)))
            ebias_ref[e] = jnp.sum(jnp.where(biases_of_devices(), spaced, 0.0), 0, keepdims=True)
        for b in range(2):
            normed, _ = norm_parts(tokens_ref[b].astype(jnp.float32))
            rows = (normed * small_ref[0:1] + small_ref[2:3]).astype(jnp.bfloat16)
            wide_ref[b] = spread_out(rows, spread_ref[...])

    weight = to_wide(core, mine_ref[...], other_ref[...])
    bias = jnp.where(j == 0, small_ref[4:5], jnp.where(j == 1, 0.0, small_ref[5:6]))
    for b in range(2):
        qkv_ref[b] = (mm(wide_ref[b], weight, ((1,), (0,))) + bias).astype(jnp.bfloat16)


def head_probs(query, key):
    scores = mm(query, key, ((1,), (1,))) * (HEAD ** (-0.5))
    return softmax_rows(scores)


def attend_kernel(
    core_ref, mine_ref, other_ref, qkv_ref, tokens_ref, routes_ref, small_ref, spread_ref,
    attended_ref, middle_ref, input_ref, prob_ref, gate_ref, kept,
):
    core = core_ref[0]
    width = tokens_ref.shape[-1]
    for pair in range(width // (2 * HEAD)):
        parts = []
        for h in (2 * pair, 2 * pair + 1):
            query, key, value = [
                qkv_ref[:, k * width + h * HEAD : k * width + (h + 1) * HEAD] for k in range(3)
            ]
            weights = head_probs(query, key).astype(jnp.bfloat16)
            parts.append(mm(weights, value, ((1,), (0,))))
        kept[:, pair * 128 : pair * 128 + 128] = jnp.concatenate(parts, 1).astype(jnp.bfloat16)
    spread = spread_ref[...]
    attended = spread_out(kept[...], spread)
    attended_ref[...] = attended
    weight = to_wide(core, mine_ref[...], other_ref[...])
    branch = mm(attended, weight, ((1,), (0,))) + small_ref[6:7]
    middle = tokens_ref[...].astype(jnp.float32) + branch
    middle_ref[...] = middle
    normed, _ = norm_parts(middle)
    rows = (normed * small_ref[1:2] + small_ref[3:4]).astype(jnp.bfloat16)
    input_ref[...] = spread_out(rows, spread)
    logits = mm(rows, small_ref[7:10].astype(jnp.bfloat16), ((1,), (1,)))
    prob = softmax_rows(logits)
    prob_ref[...] = prob
    experts = lax.broadcasted_iota(jnp.int32, prob.shape, 1)
    routes = routes_ref[...]
    member = ((experts == routes[:, 0:1]) | (experts == routes[:, 1:2])).astype(jnp.float32)
    chosen = member * prob
    gate_ref[...] = chosen / jnp.sum(chosen, 1, keepdims=True)


def expert_kernel(
    e, core_ref, w2_ref, w1_ref, b1_ref, b2_ref, x_ref, cot_ref, slot_row_ref, slot_col_ref,
    gate_ref, out_in_ref, *rest,
):
    (
        own_ref, send_ref, db1_ref, db2_ref, out_ref, dx_ref, gg_ref,
        xs, xts, rs, rows_acc, dx_acc, kept, sems,
    ) = rest[-14:]
    dx_in_ref = rest[0] if e > 0 else None
    i = pl.program_id(0)
    core = core_ref[0]
    tokens = x_ref.shape[1]

    @pl.when(i == 0)
    def _():
        taken, grads = 0.0, 0.0
        for b in range(2):
            slots = lax.broadcasted_iota(jnp.int32, (SLOTS, tokens), 0)
            pick = ones_where(slots == slot_row_ref[b, e : e + 1, :])
            taken += mm(pick, x_ref[b], ((1,), (0,)))
            scaled = (gate_ref[b][:, e : e + 1] * cot_ref[b]).astype(jnp.bfloat16)
            grads += mm(pick, scaled, ((1,), (0,)))
        xs[...] = taken.astype(jnp.bfloat16)
        xts[...] = taken.T.astype(jnp.bfloat16)
        rs[...] = grads.astype(jnp.bfloat16)
        db2_ref[...] = jnp.sum(grads, 0, keepdims=True)
        rows_acc[...] = jnp.zeros_like(rows_acc) + b2_ref[...]
        dx_acc[...] = jnp.zeros_like(dx_acc)

    x = xs[...]
    r = rs[...]
    w1 = w1_ref[...].astype(jnp.float32).reshape(1024, 768).astype(jnp.bfloat16)
    w2 = w2_ref[...].astype(jnp.float32).reshape(768, 768).astype(jnp.bfloat16)
    hidden = mm(x, w1, ((1,), (0,))) + b1_ref[...]
    act, slope = gelu_both(hidden)
    act = act.astype(jnp.bfloat16)
    rows_acc[...] += mm(act, w2, ((1,), (0,)))
    dw2 = mm(act, r, ((0,), (0,))).reshape(16, 2, 3, 8, 768)
    for c in range(2):
        kept[c, pl.ds(pl.multiple_of(16 * i, 16), 16), 4:7] = dw2[:, c].astype(jnp.bfloat16)
    dh = mm(r, w2, ((1,), (1,))) * slope
    dh = dh.astype(jnp.bfloat16)
    db1_ref[...] = jnp.sum(dh.astype(jnp.float32), 0, keepdims=True)
    dw1 = mm(xts[...], dh, ((1,), (0,))).reshape(64, 2, 1, 8, 768)
    for c in range(2):
        kept[c, :, pl.ds(i, 1)] = dw1[:, c].astype(jnp.bfloat16)
    dx_acc[...] += mm(dh, w1, ((1,), (1,)))

    def copies(step):
        parts = [
            (slice(None), pl.ds(step, 1)),
            (pl.ds(pl.multiple_of(16 * step, 16), 16), pl.ds(4, 3)),
        ]
        pairs = [(kept.at[core], own_ref), (kept.at[1 - core], send_ref)]
        return [
            pltpu.make_async_copy(source.at[part], ref.at[part], sems.at[step, 2 * k + m])
            for k, (source, ref) in enumerate(pairs)
            for m, part in enumerate(parts)
        ]

    for copy in copies(i):
        copy.start()

    @pl.when(i == pl.num_programs(0) - 1)
    def _():
        rows_terms = two_terms(rows_acc[...])
        dx_terms = two_terms(dx_acc[...])
        for b in range(2):
            slots = lax.broadcasted_iota(jnp.int32, (tokens, SLOTS), 1)
            put = ones_where(slots == slot_col_ref[b][:, e : e + 1])
            rows = sum([mm(put, term, ((1,), (0,))) for term in rows_terms])
            out_ref[b] = out_in_ref[b] + gate_ref[b][:, e : e + 1] * rows
            gg_ref[b] = jnp.sum(rows * cot_ref[b], 1, keepdims=True)
            grad = sum([mm(put, term, ((1,), (0,))) for term in dx_terms])
            dx_ref[b] = grad if e == 0 else dx_in_ref[b] + grad
        for step in range(4):
            for copy in copies(step):
                copy.wait()


def route_back_kernel(
    core_ref, mine_ref, other_ref, dx_ref, gg0_ref, gg1_ref, gg2_ref, prob_ref, gate_ref,
    slots_ref, middle_ref, cot_ref, attended_ref, small_ref, spread_ref, *rest,
):
    grad_ref, attended_grad_ref, own_ref, send_ref, small_out_ref = rest[-5:]
    core = core_ref[0]
    spread = spread_ref[...]
    weight = to_wide(core, mine_ref[...], other_ref[...])
    router = small_ref[7:10].astype(jnp.bfloat16)
    total, sums, router_grad = 0.0, [0.0, 0.0, 0.0], 0.0
    for b in range(2):
        prob, gate = prob_ref[b], gate_ref[b]
        experts = lax.broadcasted_iota(jnp.int32, prob.shape, 1)
        gate_grad = jnp.where(
            experts == 0, gg0_ref[b], jnp.where(experts == 1, gg1_ref[b], gg2_ref[b])
        )
        member = (slots_ref[b] >= 0).astype(jnp.float32)
        chosen = jnp.sum(member * prob, 1, keepdims=True)
        share = jnp.sum(gate_grad * gate, 1, keepdims=True)
        prob_grad = member * (gate_grad - share) / chosen
        logit_grad = prob * (prob_grad - jnp.sum(prob * prob_grad, 1, keepdims=True))
        logit_grad = logit_grad.astype(jnp.bfloat16)
        normed, inverse = norm_parts(middle_ref[b])
        rows = (normed * small_ref[1:2] + small_ref[3:4]).astype(jnp.bfloat16)
        router_grad += mm(logit_grad, rows, ((0,), (0,)))
        grad = pull_in(dx_ref[b], spread) + mm(logit_grad, router, ((1,), (0,)))
        sums[0] += jnp.sum(grad * normed, 0, keepdims=True)
        sums[1] += jnp.sum(grad, 0, keepdims=True)
        grad = cot_ref[b] + norm_back(grad * small_ref[1:2], normed, inverse)
        grad_ref[b] = grad
        branch = grad.astype(jnp.bfloat16)
        sums[2] += jnp.sum(branch.astype(jnp.float32), 0, keepdims=True)
        total += mm(attended_ref[b], branch, ((0,), (0,)))
        wide = mm(branch, weight, ((1,), (1,))).astype(jnp.bfloat16)
        attended_grad_ref[b] = mm(wide, spread, ((1,), (1,))).astype(jnp.bfloat16)
    by_core(core, total, own_ref, send_ref)
    for k in range(3):
        small_out_ref[k : k + 1] = sums[k]
    small_out_ref[3:6] = router_grad


def attend_back_kernel(qkv_ref, grad_ref, *rest):
    out_ref = rest[-1]
    width = grad_ref.shape[-1]
    scaling = HEAD ** (-0.5)
    for pair in range(width // (2 * HEAD)):
        parts = [[], [], []]
        for h in (2 * pair, 2 * pair + 1):
            query, key, value = [
                qkv_ref[:, k * width + h * HEAD : k * width + (h + 1) * HEAD] for k in range(3)
            ]
            grad = grad_ref[:, h * HEAD : (h + 1) * HEAD]
            probs = head_probs(query, key)
            prob_grad = mm(grad, value, ((1,), (1,)))
            score_grad = probs * (prob_grad - jnp.sum(probs * prob_grad, 1, keepdims=True))
            score_grad = score_grad.astype(jnp.bfloat16)
            parts[0].append(mm(score_grad, key, ((1,), (0,))) * scaling)
            parts[1].append(mm(score_grad, query, ((0,), (0,))) * scaling)
            parts[2].append(mm(probs.astype(jnp.bfloat16), grad, ((0,), (0,))))
        for k in range(3):
            at = k * width + pair * 128
            out_ref[:, at : at + 128] = jnp.concatenate(parts[k], 1).astype(jnp.bfloat16)


def qkv_back_kernel(
    core_ref, mine_ref, other_ref, qkv_grad0_ref, qkv_grad1_ref, wide_ref, tokens_ref, grad_ref,
    small_ref, early_ref, in0_ref, in1_ref, in2_ref, out0_ref, out1_ref, out2_ref, of_device_ref,
    spread_ref, *rest,
):
    own_ref, send_ref, small_own_ref, small_send_ref, input_grad_ref, acc, sums = rest[-7:]
    j = pl.program_id(0)
    core = core_ref[0]
    weight = to_wide(core, mine_ref[...], other_ref[...])

    @pl.when(j == 0)
    def _():
        acc[...] = jnp.zeros_like(acc)
        sums[...] = jnp.zeros_like(sums)
        sums[1:2] = early_ref[0:1]
        sums[3:4] = early_ref[1:2]
        sums[6:10] = early_ref[2:6]

    total, bias = 0.0, 0.0
    for b in range(2):
        grad = (qkv_grad0_ref, qkv_grad1_ref)[b][...]
        total += mm(wide_ref[b], grad, ((0,), (0,)))
        bias += jnp.sum(grad.astype(jnp.float32), 0, keepdims=True)
        acc[b] += mm(grad, weight, ((1,), (1,)))
    by_core(core, total, own_ref, send_ref)

    @pl.when(j == 0)
    def _():
        sums[4:5] += bias

    @pl.when(j == 2)
    def _():
        sums[5:6] += bias
        spread = spread_ref[...]
        for b in range(2):
            normed, inverse = norm_parts(tokens_ref[b].astype(jnp.float32))
            grad = pull_in(acc[b], spread)
            sums[0:1] += jnp.sum(grad * normed, 0, keepdims=True)
            sums[2:3] += jnp.sum(grad, 0, keepdims=True)
            input_grad_ref[b] = grad_ref[b] + norm_back(grad * small_ref[0:1], normed, inverse)
        small = mm(spread, sums[...].astype(jnp.bfloat16), ((0,), (1,)))
        blocks = []
        for inner, outer in ((in0_ref, out0_ref), (in1_ref, out1_ref), (in2_ref, out2_ref)):
            biases = jnp.concatenate([inner[...], outer[...]], 1)
            spaced = jnp.where(biases_of_devices(), biases, 0.0).astype(jnp.bfloat16)
            blocks.append(mm(spaced, of_device_ref[...], ((1,), (0,)))[:, :32])
        blocks.append(jnp.zeros((128, 32), jnp.float32))
        blocks = jnp.concatenate(blocks, 1).astype(jnp.bfloat16)
        small += mm(spare_rows(), blocks, ((1,), (0,)))
        by_core(core, small, small_own_ref, small_send_ref)


def pair_kernel(own_qkv, got_qkv, own_out, got_out, own_small, got_small, *rest):
    out_ref = rest[-1]
    at = 0
    for own, got in ((own_qkv, got_qkv), (own_out, got_out), (own_small, got_small)):
        total = own[...].astype(jnp.float32) + got[...].astype(jnp.float32)
        out_ref[:, :, at : at + own.shape[2]] = total.astype(jnp.bfloat16)
        at += own.shape[2]


def call(kernel, grid, ins, outs, scratch=(), after=(), flops=0):
    def spec(shape, block, index):
        if block == "any":
            return pl.BlockSpec(memory_space=pl.ANY)
        if block is None:
            return pl.BlockSpec(shape, lambda *_: (0,) * len(shape))
        return pl.BlockSpec(block, index)

    in_specs = [
        pl.BlockSpec(memory_space=pltpu.SMEM)
        if block == "smem"
        else spec(array.shape, block, index)
        for array, block, index in ins
    ]
    in_specs += [pl.BlockSpec(memory_space=pl.ANY)] * len(after)
    arrays = [array for array, _, _ in ins]
    return pl.pallas_call(
        kernel,
        grid=grid,
        in_specs=in_specs,
        out_specs=[spec(shape, block, index) for shape, _, block, index in outs],
        out_shape=[jax.ShapeDtypeStruct(shape, kind) for shape, kind, _, _ in outs],
        scratch_shapes=list(scratch),
        compiler_params=pltpu.CompilerParams(vmem_limit_bytes=58 * 1024 * 1024),
        cost_estimate=pl.CostEstimate(flops=flops, bytes_accessed=2_000_000_000, transcendentals=0),
    )(*arrays, *after)


def adam_update(weight, gradient, first_old, second_old, rate_value, decay_rate):
    first_new = BETA_ONE * first_old + (1.0 - BETA_ONE) * gradient
    second_new = BETA_TWO * second_old + (1.0 - BETA_TWO) * gradient * gradient
    weight_full = weight.astype(jnp.float32)
    ratio = (
        first_new
        / (1.0 - BETA_ONE**STEP)
        / (jnp.sqrt(second_new / (1.0 - BETA_TWO**STEP)) + ADAM_EPS)
    )
    return (first_new, second_new, weight_full - rate_value * (ratio + decay_rate * weight_full))


def on_device(
    tokens,
    cotangent,
    routes,
    qkv_weight,
    out_weight,
    norm_gain,
    bias_rows,
    router_weight,
    expand_weight,
    shrink_weight,
    expert_bias,
    *moments,
):
    f32, bf = jnp.float32, jnp.bfloat16
    core = lax.axis_index(CORE)
    core_word = (core.astype(jnp.int32).reshape(1), "smem", None)
    micro, rows, width = tokens.shape

    def all_of(array):
        return (array, None, None)

    attn_own = jnp.concatenate(
        [qkv_weight, out_weight, norm_gain.T, bias_rows.T, router_weight, jnp.zeros((6, 118), bf)], 1
    )
    ebias_own = jnp.pad(expert_bias, [(0, 0), (0, 2)]).reshape(1, 96)
    attn_own = jnp.concatenate(
        [attn_own, jnp.pad(ebias_own, [(0, 1), (3072, 32)])], 0
    )
    mine = chips_gather(attn_own).reshape(64, 8, 3200)
    other = swap_cores(mine)

    w1_own = pad_rows(expand_weight, 8).reshape(3, 8, 4, 768).transpose(0, 2, 1, 3)
    expert_own = jnp.concatenate([shrink_weight.reshape(3, 3, 8, 768), w1_own], 1)
    expert_whole = lax.all_gather(expert_own[None], DEV, axis=0, tiled=True)

    def column(array, k, n=768):
        return (array, (64, 8, n), lambda *_: (0, 0, k))

    def columns(array):
        return (array, (64, 8, 768), lambda j: (0, 0, j))

    hot = (routes[:, :, :, None] == jnp.arange(3, dtype=jnp.int32)).astype(f32)
    member = jnp.sum(hot, 2).reshape(micro * rows, 3)
    lower = jnp.arange(micro * rows)[:, None] >= jnp.arange(micro * rows)[None, :]
    position = jnp.dot(lower.astype(bf), member.astype(bf), preferred_element_type=f32) - 1.0
    slots = jnp.where(member > 0, position, -1.0).astype(jnp.int32).reshape(micro, rows, 3)
    slot_rows = slots.transpose(0, 2, 1)

    spread = (
        (jnp.arange(width) // 6 * 8 + jnp.arange(width) % 6)[:, None] == jnp.arange(1024)[None, :]
    ).astype(bf)

    of_device = (jnp.arange(3840)[:, None] % 30 == jnp.arange(128)[None, :]).astype(bf)

    qkv, attn_wide, small, ebias = call(
        qkv_kernel,
        (3,),
        [
            core_word, columns(mine), columns(other), column(mine, 24, 128),
            column(other, 24, 128), all_of(spread), all_of(tokens), all_of(of_device),
        ],
        [
            ((micro, rows, 3 * width), bf, (micro, rows, 768), lambda j: (0, 0, j)),
            ((micro, rows, 1024), bf, None, None),
            ((128, width), f32, None, None),
            ((3, 1, 3840), f32, None, None),
        ],
        flops=2 * 394 * 1024 * 3000,
    )

    def one(array):
        return (array, (None, *array.shape[1:]), lambda b: (b, 0, 0))

    def one_out(n, kind):
        return ((micro, rows, n), kind, (None, rows, n), lambda b: (b, 0, 0))

    attended, middle, expert_input, prob, gates = call(
        attend_kernel,
        (micro,),
        [
            core_word, column(mine, 3), column(other, 3), one(qkv), one(tokens), one(routes),
            all_of(small), all_of(spread),
        ],
        [
            one_out(1024, bf), one_out(width, f32), one_out(1024, bf), one_out(3, f32),
            one_out(3, f32),
        ],
        [pltpu.VMEM((rows, width), bf)],
        flops=2 * 394 * 1024 * 2400,
    )

    output = middle
    wide_grad = None
    gate_grads, inner, outer, rings = [], [], [], []

    follow = ()
    for e in range(3):
        own, send, db1, db2, output, wide_grad, gg = call(
            functools.partial(expert_kernel, e),
            (4,),
            [
                core_word,
                (expert_whole, (32, None, 3, 8, 768), lambda i, e=e: (i, e, 0, 0, 0)),
                (expert_whole, (128, None, 1, 8, 768), lambda i, e=e: (0, e, 3 + i, 0, 0)),
                (ebias, (None, 1, 768), lambda i, e=e: (e, 0, i)),
                (ebias, (None, 1, 768), lambda i, e=e: (e, 0, 4)),
                all_of(expert_input), all_of(cotangent), all_of(slot_rows), all_of(slots),
                all_of(gates), all_of(output),
            ]
            + ([all_of(wide_grad)] if e else []),
            [
                ((64, 7, 8, 768), bf, "any", None),
                ((64, 7, 8, 768), bf, "any", None),
                ((1, 3072), f32, (1, 768), lambda i: (0, i)),
                ((1, 768), f32, None, None),
                ((micro, rows, width), f32, None, None),
                ((micro, rows, 1024), f32, None, None),
                ((micro, rows, 1), f32, None, None),
            ],
            [
                pltpu.VMEM((SLOTS, 1024), bf),
                pltpu.VMEM((1024, SLOTS), bf),
                pltpu.VMEM((SLOTS, 768), bf),
                pltpu.VMEM((SLOTS, 768), f32),
                pltpu.VMEM((SLOTS, 1024), f32),
                pltpu.VMEM((2, 64, 7, 8, 768), bf),
                pltpu.SemaphoreType.DMA((4, 4)),
            ],
            after=follow,
            flops=6 * 2 * SLOTS * 900 * 3072,
        )
        gate_grads.append(gg)
        inner.append(db1)
        outer.append(db2)
        if e == 1:
            *follow, send = next_round(rings, (gg,), (send,))
        elif e == 2:
            *follow, send = next_round(rings, (gg,), (send,))
        rings.append(Ring((own, swap_cores(send)), *((0, 1), (1, 2), (2, 1))[e]))

    middle_grad, attended_grad, own_out, send_out, small_grad = call(
        route_back_kernel,
        (1,),
        [
            core_word, column(mine, 3), column(other, 3), all_of(wide_grad),
            all_of(gate_grads[0]), all_of(gate_grads[1]), all_of(gate_grads[2]), all_of(prob),
            all_of(gates), all_of(slots), all_of(middle), all_of(cotangent), all_of(attended),
            all_of(small),
            all_of(spread),
        ],
        [
            ((micro, rows, width), f32, None, None),
            ((micro, rows, width), bf, None, None),
            ((64, 8, 768), bf, None, None),
            ((64, 8, 768), bf, None, None),
            ((8, width), f32, None, None),
        ],
        after=follow,
        flops=2 * 394 * 1024 * 4000,
    )
    qkv_grads = []
    follow = next_round(rings, (small_grad,))
    for b in range(micro):
        qkv_grads.append(
            call(
                attend_back_kernel,
                (1,),
                [
                    (qkv, (None, rows, 3 * width), lambda _, b=b: (b, 0, 0)),
                    (attended_grad, (None, rows, width), lambda _, b=b: (b, 0, 0)),
                ],
                [((rows, 3 * width), bf, None, None)],
                after=qkv_grads if b else follow,
                flops=2 * 197 * 1024 * 4000,
            )[0]
        )
    next_round(rings, qkv_grads[1:])
    follow = next_round(rings[:1])
    own_qkv, send_qkv, own_small, send_small, input_grad = call(
        qkv_back_kernel,
        (3,),
        [
            core_word, columns(mine), columns(other),
            *[(grad, (rows, 768), lambda j: (0, j)) for grad in qkv_grads],
            all_of(attn_wide), all_of(tokens), all_of(middle_grad), all_of(small),
            all_of(small_grad), *[all_of(a) for a in inner], *[all_of(a) for a in outer],
            all_of(of_device), all_of(spread),
        ],
        [
            ((64, 8, 3 * width), bf, (64, 8, 768), lambda j: (0, 0, j)),
            ((64, 8, 3 * width), bf, (64, 8, 768), lambda j: (0, 0, j)),
            ((64, 8, 128), bf, None, None),
            ((64, 8, 128), bf, None, None),
            ((micro, rows, width), f32, None, None),
        ],
        [pltpu.VMEM((micro, rows, 1024), f32), pltpu.VMEM((128, width), f32)],
        after=follow,
        flops=2 * 394 * 1024 * 5000,
    )

    follow = next_round(rings, (own_small,))
    def chips_part(n):
        return (16, 8, n), lambda i: (i, 0, 0)

    parts = ((own_qkv, send_qkv), (own_out, send_out), (own_small, send_small))
    pair = call(
        pair_kernel,
        (4,),
        [
            (a, *chips_part(own.shape[2])) for own, send in parts for a in (own, swap_cores(send))
        ],
        [((64, 8, 3200), bf, *chips_part(3200))],
        after=follow,
    )[0]
    rings.append(Ring((pair,), 0))
    next_round(rings)
    next_round(rings)
    expert_sums = [rings[0].total()]
    next_round(rings[1:])
    next_round(rings[1:], expert_sums[:1])
    attn_sum = rings[3].total()
    next_round(rings[2:3])
    expert_sums += totals(rings[1:3])
    ebias_sum = attn_sum[6, 3072:3168].reshape(3, 32)[:, :30]
    attn_sum = attn_sum[:6]
    small_sum = attn_sum[:, 3072:]
    gain_sum, shift_sum, router_sum = small_sum[:, :2].T, small_sum[:, 2:7].T, small_sum[:, 7:10]
    expert_sums = jnp.stack(expert_sums)
    expand_sum = expert_sums[:, :4, :6].transpose(0, 2, 1, 3).reshape(3, 6, 3072)
    shrink_sum = expert_sums[:, 4:].reshape(3, 24, 768)

    weights_all = (
        qkv_weight,
        out_weight,
        norm_gain,
        bias_rows,
        router_weight,
        expand_weight,
        shrink_weight,
        expert_bias,
    )
    grads_all = (
        attn_sum[:, :2304],
        attn_sum[:, 2304:3072],
        gain_sum,
        shift_sum,
        router_sum,
        expand_sum,
        shrink_sum,
        ebias_sum,
    )
    results = [output, input_grad]
    for k in range(8):
        results.extend(
            adam_update(
                weights_all[k], grads_all[k], moments[k], moments[8 + k], RATES[k], DECAYS[k]
            )
        )
    return tuple(results)


def solution(mesh):
    split = Mesh(mesh.devices.reshape(4, 4, 4, 2), ("dev_0", "dev_1", "dev_2", "dev_3"))
    placed = (
        P(None, DEV, None),
        P(None, DEV, None),
        P(None, DEV, None),
        P(DEV, None),
        P(DEV, None),
        P(None, DEV),
        P(None, DEV),
        P(DEV, None),
        P(None, DEV, None),
        P(None, DEV, None),
        P(None, DEV),
        P(DEV, None),
        P(DEV, None),
        P(None, DEV),
        P(None, DEV),
        P(DEV, None),
        P(None, DEV, None),
        P(None, DEV, None),
        P(None, DEV),
        P(DEV, None),
        P(DEV, None),
        P(None, DEV),
        P(None, DEV),
        P(DEV, None),
        P(None, DEV, None),
        P(None, DEV, None),
        P(None, DEV),
    )
    return jax.shard_map(
        on_device,
        mesh=split,
        in_specs=placed,
        out_specs=(
            P(None, DEV, None),
            P(None, DEV, None),
            P(DEV, None),
            P(DEV, None),
            P(DEV, None),
            P(DEV, None),
            P(DEV, None),
            P(DEV, None),
            P(None, DEV),
            P(None, DEV),
            P(None, DEV),
            P(None, DEV),
            P(None, DEV),
            P(None, DEV),
            P(DEV, None),
            P(DEV, None),
            P(DEV, None),
            P(None, DEV, None),
            P(None, DEV, None),
            P(None, DEV, None),
            P(None, DEV, None),
            P(None, DEV, None),
            P(None, DEV, None),
            P(None, DEV),
            P(None, DEV),
            P(None, DEV),
        ),
        check_vma=False,
    )
```
